32 devices in a mesh: img: 16 (over z, y, x), grp: 2 (over core).
Axes of the slice: x: 2, y: 2, z: 4, core: 2. Of those that a mesh axis runs over, the one named last changes fastest.
Arguments:
- tokens: bfloat16 [512, 8, 1024], P('img'), may hold values from -16 to 16
- w_embed: bfloat16 [1024, 768], replicated, may hold values from -0.1875 to 0.1875
- w_query: bfloat16 [768, 768], replicated, may hold values from -1 to 1
- w_key: bfloat16 [768, 768], replicated, may hold values from -1 to 1
- w_value: bfloat16 [768, 768], replicated, may hold values from -0.21875 to 0.21875
- w_out: bfloat16 [768, 768], replicated, may hold values from -0.21875 to 0.21875
- w_head: bfloat16 [768, 28], replicated, may hold values from -0.109375 to 0.109375
- pair_images: int32 [16, 2, 64, 2], replicated, may hold values from 0 to 511, as said below
- pair_counts: int32 [16, 2], replicated, may hold values from 48 to 64, as said below
- owner_row: int32 [512], replicated, may hold values from 0 to 511, as said below
Outputs:
- joined_geometry: float32 [512, 32], P('img')
- joined_descriptors: float32 [512, 192], P('img')
The draws below stay inside these ranges and needn't reach their ends.
Inputs may be any that keep to these rules, and one draw needn't show every extreme that they name: `pair_images`: the owner of an image is owner_row of it integer-divided by 32. Among the 256 views of the pair slots of one chip (both cores, live or not), no owner holds more than 16; in every draw some owner holds exactly 16 live ones of some chip. The two images of a pair have different owners. `pair_counts`: slots at or beyond the count are ignored; some executor has 64. `owner_row`: A permutation.
All inputs are finite; a program needn't handle non-finite values.
Results may differ from the reference program's by a relative error of at most 0.0065.
Values may be sent and summed in bfloat16 or wider, within the bound.
A program may use at most 64 MiB of HBM per device.

```python
import math
import jax
import jax.numpy as jnp
from jax import lax

ENC = 1024
DEC = 768
HEADS = 12
CH = 28
PATCHES = 8
IMG_DEV = 32
PAIR_CAP = 64
OWNERS = 16
GROUPS = 2
IMAGES = 512
SLOT = 16


def shared_layout(key):
    perm_key, owner_key, offset_key = jax.random.split(jax.random.fold_in(key, 101), 3)
    owner_row = jax.random.permutation(perm_key, IMAGES).astype(jnp.int32)
    end_count = GROUPS * PAIR_CAP * 2
    half_count = GROUPS * PAIR_CAP
    groups_needed = (end_count + SLOT - 1) // SLOT
    noise_bits = jax.random.randint(owner_key, (OWNERS, OWNERS), 0, 1 << 20)
    owner_order = jnp.argsort(noise_bits * OWNERS + jnp.arange(OWNERS, dtype=jnp.int32)[None, :], axis=1).astype(jnp.int32)
    position = jnp.arange(end_count, dtype=jnp.int32)
    ordered = position % 2 * half_count + position // 2
    member = ordered // SLOT
    chosen = owner_order[:, member]
    offsets = jax.random.randint(offset_key, (OWNERS, groups_needed), 0, IMG_DEV)
    within = (offsets[:, member] + ordered % SLOT) % IMG_DEV
    token_rows = chosen * IMG_DEV + within
    inverse = jnp.zeros((IMAGES,), jnp.int32).at[owner_row].set(jnp.arange(IMAGES, dtype=jnp.int32))
    images = inverse[token_rows].reshape(OWNERS, GROUPS, PAIR_CAP, 2)
    return (owner_row, images.astype(jnp.int32))


def draw_owner_row(key, part):
    return shared_layout(key)[0]


def draw_pair_images(key, part):
    return shared_layout(key)[1]


def draw_pair_counts(key, part):
    key = jax.random.fold_in(key, 13)
    count_key, chip_key, core_key = jax.random.split(key, 3)
    fewest = 3 * PAIR_CAP // 4
    counts = jax.random.randint(count_key, (OWNERS, GROUPS), fewest, PAIR_CAP + 1)
    busy_chip = jax.random.randint(chip_key, (), 0, OWNERS)
    busy_core = jax.random.randint(core_key, (), 0, GROUPS)
    is_busy = (jnp.arange(OWNERS)[:, None] == busy_chip) & (jnp.arange(GROUPS)[None, :] == busy_core)
    return jnp.where(is_busy, PAIR_CAP, counts).astype(jnp.int32)


def draw_tokens(key, part):
    key = jax.random.fold_in(key, 17)
    base_key, row_key, col_key = jax.random.split(key, 3)
    shape = (IMAGES, PATCHES, ENC)
    row_scale = jnp.exp(jax.random.uniform(row_key, (IMAGES, PATCHES, 1), minval=math.log(0.5), maxval=math.log(5.0)))
    col_scale = jnp.exp(jax.random.uniform(col_key, (1, 1, ENC), minval=math.log(0.5), maxval=math.log(5.0)))
    drawn = jax.random.normal(base_key, shape) * row_scale * col_scale / 4.0
    return jnp.clip(drawn, -16.0, 16.0).astype(jnp.bfloat16)


def draw_w_query(key, part):
    own_key = jax.random.fold_in(key, 43)
    own_part = jax.random.normal(own_key, (DEC, DEC))
    return jnp.clip(own_part / math.sqrt(DEC), -1.0, 1.0).astype(jnp.bfloat16)


def draw_w_key(key, part):
    own_key = jax.random.fold_in(key, 47)
    own_part = jax.random.normal(own_key, (DEC, DEC))
    return jnp.clip(own_part / math.sqrt(DEC), -1.0, 1.0).astype(jnp.bfloat16)


def gaussian(rng, extent, width, reach, held_as=jnp.bfloat16):
    values = width * jax.random.normal(rng, extent, jnp.float32)
    return jnp.clip(values, min=-reach, max=reach).astype(held_as)


def setup_inputs(seed: int = 0) -> dict:
    keys = jax.random.split(jax.random.key(seed), 11)
    tokens = draw_tokens(jax.random.fold_in(keys[10], 71), 0)
    w_embed = gaussian(keys[1], (ENC, DEC), ENC ** -0.5, 0.1875)
    w_query = draw_w_query(jax.random.fold_in(keys[10], 71), 0)
    w_key = draw_w_key(jax.random.fold_in(keys[10], 71), 0)
    w_value = gaussian(keys[4], (DEC, DEC), DEC ** -0.5, 0.21875)
    w_out = gaussian(keys[5], (DEC, DEC), DEC ** -0.5, 0.21875)
    w_head = gaussian(keys[6], (DEC, CH), (4 * DEC) ** -0.5, 0.109375)
    pair_images = draw_pair_images(jax.random.fold_in(keys[10], 71), 0)
    pair_counts = draw_pair_counts(jax.random.fold_in(keys[10], 71), 0)
    owner_row = draw_owner_row(jax.random.fold_in(keys[10], 71), 0)
    return dict(tokens=tokens, w_embed=w_embed, w_query=w_query, w_key=w_key, w_value=w_value, w_out=w_out, w_head=w_head, pair_images=pair_images, pair_counts=pair_counts, owner_row=owner_row)


def rounded(values):
    return lax.optimization_barrier(values.astype(jnp.bfloat16))

def layer_norm(values):
    center = values - lax.optimization_barrier(jnp.mean(values, axis=-1, keepdims=True))
    spread = lax.optimization_barrier(jnp.mean(center * center, axis=-1, keepdims=True))
    return center * lax.rsqrt(spread + 1e-05)

def contribution(head_out):
    confidence = 1.0 + jnp.exp(head_out[..., 3:4, :])
    return jnp.concatenate([confidence * head_out[..., :3, :], confidence, confidence * head_out[..., 4:, :]], axis=-2)

def join(totals, patches, channels):
    image_count = totals.shape[0]
    shaped = totals.reshape(image_count, channels, patches)
    confidence = shaped[:, 3:4, :]
    geometry = jnp.concatenate([shaped[:, :3, :] / (1.0 + confidence), jnp.log1p(confidence)], axis=1)
    descriptors = shaped[:, 4:, :] / (1.0 + confidence)
    return (geometry.reshape(image_count, 4 * patches), descriptors.reshape(image_count, (channels - 4) * patches))

def reference(tokens, w_embed, w_query, w_key, w_value, w_out, w_head, pair_images, pair_counts, owner_row):
    images_all, patches, enc_width = tokens.shape
    dec_width = w_query.shape[0]
    channels = w_head.shape[1]
    head_size = dec_width // HEADS
    flat_tokens = tokens.reshape(images_all * patches, enc_width)
    embedded = rounded(jnp.dot(flat_tokens, w_embed, preferred_element_type=jnp.float32))
    normed = rounded(layer_norm(embedded.astype(jnp.float32)))
    queries = rounded(jnp.dot(normed, w_query, preferred_element_type=jnp.float32)).reshape(images_all, patches, HEADS, head_size)
    key_proj = rounded(jnp.dot(normed, w_key, preferred_element_type=jnp.float32)).reshape(images_all, patches, HEADS, head_size)
    value_proj = rounded(jnp.dot(normed, w_value, preferred_element_type=jnp.float32)).reshape(images_all, patches, HEADS, head_size)
    embedded = embedded.reshape(images_all, patches, dec_width)
    token_rows = owner_row[pair_images].reshape(-1, PAIR_CAP, 2).astype(jnp.int32)
    out_weight = w_out.astype(jnp.float32)
    head_weight = w_head.astype(jnp.float32)

    def one_block(block_rows):
        partner = block_rows[:, ::-1]
        query_blk = queries[block_rows].astype(jnp.float32)
        key_blk = key_proj[partner].astype(jnp.float32)
        value_blk = value_proj[partner].astype(jnp.float32)
        scores = jnp.einsum('sxphd,sxqhd->sxhpq', query_blk, key_blk) / math.sqrt(head_size)
        weights = rounded(jax.nn.softmax(scores, axis=-1)).astype(jnp.float32)
        attended = rounded(jnp.einsum('sxhpq,sxqhd->sxphd', weights, value_blk))
        attended = attended.astype(jnp.float32).reshape(PAIR_CAP, 2, patches, dec_width)
        mixed_rows = embedded[block_rows].astype(jnp.float32) + jnp.einsum('sxpd,de->sxpe', attended, out_weight)
        mixed_rows = rounded(mixed_rows).astype(jnp.float32)
        head_out = jnp.einsum('sxpd,dc->sxcp', mixed_rows, head_weight)
        return contribution(head_out).reshape(PAIR_CAP, 2, channels * patches)
    results = lax.map(one_block, token_rows)
    is_live = (jnp.arange(PAIR_CAP, dtype=jnp.int32)[None, None, :] < pair_counts[:, :, None]).reshape(-1, PAIR_CAP)
    results = results * is_live[:, :, None, None].astype(jnp.float32)
    totals = jnp.zeros((images_all, channels * patches), jnp.float32)
    totals = totals.at[token_rows.reshape(-1)].add(results.reshape(-1, channels * patches))
    return join(totals, patches, channels)
```

```python
import functools
import math

import jax
import jax.numpy as jnp
from jax import lax
from jax.experimental import pallas as pl
from jax.experimental.pallas import tpu as pltpu
from jax.sharding import PartitionSpec as P

HEADS = 12
PAIR_BLOCK = 8
GATHER_LIMIT = 16 * 2**20
TABLE = 128
LANES = 128


def layer_norm(values):
    center = values - jnp.mean(values, axis=-1, keepdims=True)
    spread = jnp.mean(center * center, axis=-1, keepdims=True)
    return center * lax.rsqrt(spread + 1e-05)


def contribution(head_out):
    confidence = 1.0 + jnp.exp(head_out[..., 3:4, :])
    return jnp.concatenate(
        [confidence * head_out[..., :3, :], confidence, confidence * head_out[..., 4:, :]], axis=-2
    )


def join(totals, patches, channels):
    image_count = totals.shape[0]
    shaped = totals.reshape(image_count, channels, patches)
    confidence = shaped[:, 3:4, :]
    geometry = jnp.concatenate(
        [shaped[:, :3, :] / (1.0 + confidence), jnp.log1p(confidence)], axis=1
    )
    descriptors = shaped[:, 4:, :] / (1.0 + confidence)
    return (
        geometry.reshape(image_count, 4 * patches),
        descriptors.reshape(image_count, (channels - 4) * patches),
    )


def decode_block(embedded, w_query, w_key, w_value, w_out, w_head):
    blocks, side_count, patches, dec_width = embedded.shape
    head_size = dec_width // HEADS
    normed = layer_norm(embedded.astype(jnp.float32)).astype(jnp.bfloat16)

    def project(weight):
        projected = jnp.einsum("bspd,de->bspe", normed, weight, preferred_element_type=jnp.float32)
        return projected.astype(jnp.bfloat16).reshape(blocks, side_count, patches, HEADS, head_size)

    queries = project(w_query)
    key_proj = project(w_key)[:, ::-1]
    value_proj = project(w_value)[:, ::-1]
    scores = jnp.einsum(
        "bsphd,bsqhd->bshpq", queries, key_proj, preferred_element_type=jnp.float32
    ) / math.sqrt(head_size)
    weights = jax.nn.softmax(scores, axis=-1).astype(jnp.bfloat16)
    attended = jnp.einsum(
        "bshpq,bsqhd->bsphd", weights, value_proj, preferred_element_type=jnp.float32
    )
    attended = attended.astype(jnp.bfloat16).reshape(blocks, side_count, patches, dec_width)
    mixed_rows = embedded.astype(jnp.float32) + jnp.einsum(
        "bspd,de->bspe", attended, w_out, preferred_element_type=jnp.float32
    )
    mixed_rows = mixed_rows.astype(jnp.bfloat16)
    head_out = jnp.einsum("bspd,dc->bscp", mixed_rows, w_head, preferred_element_type=jnp.float32)
    return contribution(head_out).reshape(blocks, side_count, -1)


def by_executor(
    tokens, w_embed, w_query, w_key, w_value, w_out, w_head, pair_images, pair_counts, owner_row
):
    img_dev, patches, enc_width = tokens.shape
    channels = w_head.shape[1]
    owners = lax.axis_size("img")
    groups = lax.axis_size("grp")
    pair_cap = pair_images.shape[2]
    slot_cap = max(2, (2 * groups * pair_cap + owners - 1) // owners)
    my_chip = lax.axis_index("img")
    my_group = lax.axis_index("grp")
    end_count = groups * pair_cap * 2
    token_rows = owner_row[pair_images].reshape(owners, end_count)
    source_owner = token_rows // img_dev
    local_row = token_rows % img_dev
    end_index = jnp.arange(end_count, dtype=jnp.int32)
    earlier = end_index[None, :] < end_index[:, None]
    same_owner = source_owner[:, :, None] == source_owner[:, None, :]
    ranked = jnp.sum((same_owner & earlier[None]).astype(jnp.int32), axis=2)
    is_live = jnp.arange(pair_cap, dtype=jnp.int32)[None, None, :] < pair_counts[:, :, None]
    group_table = jnp.broadcast_to(jnp.arange(groups, dtype=jnp.int32)[:, None], (groups, pair_cap))
    slot_table = jnp.broadcast_to(
        jnp.arange(pair_cap, dtype=jnp.int32)[None, :], (groups, pair_cap)
    )
    dest_group = jnp.broadcast_to(group_table.reshape(1, -1), (owners, groups * pair_cap))
    dest_slot = jnp.broadcast_to(slot_table.reshape(1, -1), (owners, groups * pair_cap))
    my_share = pair_counts[my_chip, my_group]
    live_end = jnp.repeat(is_live.reshape(owners, -1), 2, axis=1)
    group_end = jnp.repeat(dest_group, 2, axis=1)
    slot_end = jnp.repeat(dest_slot, 2, axis=1)
    side_end = end_index % 2
    to_send = live_end & (group_end == my_group) & (source_owner == my_chip)
    slot_index = jnp.arange(slot_cap, dtype=jnp.int32)
    matched = to_send[:, None, :] & (ranked[:, None, :] == slot_index[None, :, None])
    send_index = jnp.sum(jnp.where(matched, local_row[:, None, :], 0), axis=2)
    send_valid = jnp.any(matched, axis=2)
    mine = live_end[my_chip] & (group_end[my_chip] == my_group)
    pair_index = jnp.arange(pair_cap, dtype=jnp.int32)
    side_index = jnp.arange(2, dtype=jnp.int32)
    wanted = mine[None, None, :] & (slot_end[my_chip][None, None, :] == pair_index[:, None, None])
    wanted = wanted & (side_end[None, None, :] == side_index[None, :, None])
    flat_source = source_owner[my_chip] * slot_cap + ranked[my_chip]
    recv_index = jnp.sum(jnp.where(wanted, flat_source[None, None, :], 0), axis=2)
    recv_valid = jnp.any(wanted, axis=2)
    send_mask = send_valid[:, :, None, None].astype(jnp.bfloat16)
    embedded_own = jnp.dot(
        tokens.reshape(img_dev * patches, enc_width), w_embed, preferred_element_type=jnp.float32
    )
    embedded_own = embedded_own.astype(jnp.bfloat16).reshape(img_dev, patches, -1)
    outgoing = embedded_own[send_index] * send_mask
    received = lax.all_to_all(outgoing, "img", split_axis=0, concat_axis=0, tiled=True)
    pair_views = received.reshape(owners * slot_cap, patches, -1)[recv_index]

    def run_block(index_block, totals):
        first_row = index_block * PAIR_BLOCK
        block_views = lax.dynamic_slice_in_dim(pair_views, first_row, PAIR_BLOCK, 0)
        block_result = decode_block(block_views, w_query, w_key, w_value, w_out, w_head)
        return lax.dynamic_update_slice_in_dim(totals, block_result, first_row, 0)

    block_count = (my_share + PAIR_BLOCK - 1) // PAIR_BLOCK
    results = lax.fori_loop(
        0, block_count, run_block, jnp.zeros((pair_cap, 2, channels * patches), jnp.float32)
    )
    results = results * recv_valid[:, :, None].astype(jnp.float32)
    return_map = (
        jnp.arange(owners * slot_cap, dtype=jnp.int32)[:, None] == recv_index.reshape(1, -1)
    ) & recv_valid.reshape(1, -1)
    outgoing_back = jnp.dot(
        return_map.astype(jnp.float32),
        results.reshape(pair_cap * 2, -1),
        precision=lax.Precision.HIGHEST,
        preferred_element_type=jnp.float32,
    )
    returned = lax.all_to_all(
        outgoing_back.reshape(owners, slot_cap, -1), "img", split_axis=0, concat_axis=0, tiled=True
    )
    owner_map = (
        jnp.arange(img_dev, dtype=jnp.int32)[:, None] == send_index.reshape(1, -1)
    ) & send_valid.reshape(1, -1)
    owner_partial = jnp.dot(
        owner_map.astype(jnp.float32),
        returned.reshape(owners * slot_cap, -1),
        precision=lax.Precision.HIGHEST,
        preferred_element_type=jnp.float32,
    )
    totals = lax.psum(owner_partial, "grp")
    return join(totals, patches, channels)


def split3(values):
    high = values.astype(jnp.bfloat16)
    rest = values - high.astype(jnp.float32)
    middle = rest.astype(jnp.bfloat16)
    low = (rest - middle.astype(jnp.float32)).astype(jnp.bfloat16)
    return jnp.concatenate([high, middle, low], axis=0)


def sum3(values):
    part = values.shape[0] // 3
    return values[:part] + values[part : 2 * part] + values[2 * part :]


NT = (((1,), (1,)), ((), ()))


def decode_kernel(
    heads, source_ref, local_ref, normed_ref, query_ref, key_ref, value_ref, base_ref, place_ref,
    live_ref, out_ref, partner_rows, query_rows, attended
):
    ends = source_ref.shape[0]
    patches, width = normed_ref.shape[1:]
    channels = base_ref.shape[0]
    head_size = width // heads
    rows = ends * patches

    def fetch(end, carry):
        at = pl.ds(pl.multiple_of(end * patches, patches), patches)
        own = pl.ds(pl.multiple_of(local_ref[end] * patches, patches), patches)
        partner_rows[at, :] = normed_ref[source_ref[end]].astype(jnp.float32)
        query_rows[at, :] = query_ref[own, :]
        return carry

    lax.fori_loop(0, ends, fetch, 0, unroll=8)

    chunk = min(256, rows)
    group = LANES
    side = LANES // head_size
    lane = lax.broadcasted_iota(jnp.int32, (group, LANES), 1)
    column = lax.broadcasted_iota(jnp.int32, (patches, side * group), 1)
    column_end = (column % group) // patches

    def one_chunk(index, carry):
        first = pl.multiple_of(index * chunk, chunk)
        partner = partner_rows[pl.ds(first, chunk), :].astype(jnp.bfloat16)
        keys = jnp.dot(partner, key_ref[...], preferred_element_type=jnp.float32)
        keys = keys.astype(jnp.bfloat16)
        values = lax.dot_general(
            value_ref[...], partner, NT, preferred_element_type=jnp.float32
        ).astype(jnp.bfloat16)
        for part in range(chunk // group):
            begin = part * group
            all_weights = []
            all_values = []
            for block in range(width // LANES):
                cols = slice(block * LANES, (block + 1) * LANES)
                asked = query_rows[pl.ds(first + begin, group), cols]
                stacked = jnp.concatenate(
                    [jnp.where(lane // head_size == s, asked, 0.0) for s in range(side)], axis=0
                ).astype(jnp.bfloat16)
                scores = lax.dot_general(
                    keys[begin : begin + group, cols], stacked, NT,
                    preferred_element_type=jnp.float32,
                )
                packed = jnp.zeros((patches, side * group), jnp.float32)
                for end in range(group // patches):
                    packed = jnp.where(
                        column_end == end, scores[end * patches : (end + 1) * patches], packed
                    )
                grown = jnp.exp(packed - jnp.max(packed, axis=0, keepdims=True))
                weights = grown / jnp.sum(grown, axis=0, keepdims=True)
                spread = jnp.concatenate(
                    [jnp.where(column_end == end, weights, 0.0) for end in range(group // patches)],
                    axis=0,
                ).astype(jnp.bfloat16)
                for s in range(side):
                    head = block * side + s
                    all_weights.append(spread[:, s * group : (s + 1) * group])
                    all_values.append(
                        values[head * channels : (head + 1) * channels, begin : begin + group]
                    )
            attended[:, pl.ds(pl.multiple_of(first + begin, group), group)] = jnp.dot(
                jnp.concatenate(all_values, axis=1),
                jnp.concatenate(all_weights, axis=0),
                preferred_element_type=jnp.float32,
            )
        return carry

    lax.fori_loop(0, rows // chunk, one_chunk, 0)

    own_rows = base_ref.shape[1]
    target = lax.broadcasted_iota(jnp.int32, (own_rows, rows), 0)
    owner_map = jnp.where(target == place_ref[...], 1.0, 0.0).astype(jnp.bfloat16)
    base = sum3(jnp.dot(split3(base_ref[...]), owner_map, preferred_element_type=jnp.float32))
    head_out = base + attended[...]
    confidence = 1.0 + jnp.exp(head_out[3:4, :])
    channel = lax.broadcasted_iota(jnp.int32, head_out.shape, 0)
    result = jnp.where(channel == 3, confidence, confidence * head_out)
    result = jnp.where(live_ref[...] > 0, result, 0.0)
    out_ref[...] = sum3(
        lax.dot_general(split3(result), owner_map, NT, preferred_element_type=jnp.float32)
    )


def look_up(owner_row, ids, img_dev):
    span = min(TABLE, owner_row.shape[0])
    table = owner_row.reshape(-1, span)
    parts = jnp.concatenate([table // img_dev, table % img_dev], axis=0).astype(jnp.bfloat16)
    hot = ids[None, :] % span == jnp.arange(span, dtype=jnp.int32)[:, None]
    found = jnp.dot(parts, hot.astype(jnp.bfloat16), preferred_element_type=jnp.float32)
    found = found.reshape(2, -1, ids.shape[0])
    pick = jnp.arange(found.shape[1], dtype=jnp.int32)[:, None] == ids[None, :] // span
    found = jnp.sum(jnp.where(pick[None], found, 0.0), axis=1).astype(jnp.int32)
    return found[0], found[1]


def by_owner(
    tokens, w_embed, w_query, w_key, w_value, w_out, w_head, pair_images, pair_counts, owner_row
):
    img_dev, patches, enc_width = tokens.shape
    dec_width, channels = w_head.shape
    owners = lax.axis_size("img")
    groups = lax.axis_size("grp")
    pair_cap = pair_images.shape[2]
    my_chip = lax.axis_index("img")
    my_group = lax.axis_index("grp")
    head_size = dec_width // HEADS
    own_rows = img_dev * patches
    share = img_dev // groups
    embedded = jnp.dot(
        tokens.reshape(own_rows, enc_width), w_embed, preferred_element_type=jnp.float32
    ).astype(jnp.bfloat16)
    normed = layer_norm(embedded.astype(jnp.float32)).astype(jnp.bfloat16)
    outgoing = lax.dynamic_slice_in_dim(
        normed.reshape(img_dev, patches, dec_width), my_group * share, share, 0
    )
    everyone = lax.all_gather(outgoing, ("img", "grp"), axis=0, tiled=True)

    queries = jnp.dot(normed, w_query, preferred_element_type=jnp.float32)
    queries = queries.astype(jnp.bfloat16).astype(jnp.float32) / math.sqrt(head_size)
    wide = -(-channels // 8) * 8
    head_weight = jnp.pad(w_head, ((0, 0), (0, wide - channels)))
    base = lax.dot_general(
        head_weight, embedded, (((0,), (1,)), ((), ())), preferred_element_type=jnp.float32
    )
    out_head = jnp.dot(w_out, head_weight, preferred_element_type=jnp.float32)
    value_head = jnp.einsum(
        "hdc,ihd->hci",
        out_head.reshape(HEADS, head_size, wide),
        w_value.astype(jnp.float32).reshape(dec_width, HEADS, head_size),
        precision=lax.Precision.HIGHEST,
        preferred_element_type=jnp.float32,
    )
    value_head = value_head.reshape(HEADS * wide, dec_width).astype(jnp.bfloat16)

    end_count = groups * pair_cap * 2
    sides = [pair_images[..., s].reshape(owners, groups * pair_cap) for s in range(2)]
    ids = jnp.concatenate(sides, axis=1)
    owner, local = look_up(owner_row, ids.reshape(-1), img_dev)
    owner = owner.reshape(owners, end_count)
    local = local.reshape(owners, end_count)
    image_row = owner * img_dev + local
    half = end_count // 2
    partner = jnp.concatenate([image_row[:, half:], image_row[:, :half]], axis=1)
    live = jnp.arange(pair_cap, dtype=jnp.int32)[None, None, :] < pair_counts[:, :, None]
    live = live.reshape(owners, half).astype(jnp.int32)
    live = jnp.concatenate([live, live], axis=1)
    packed = (partner * img_dev + local) * 2 + live
    mine = owner == my_chip
    end_index = jnp.arange(end_count, dtype=jnp.int32)
    earlier = (end_index[:, None] < end_index[None, :]).astype(jnp.bfloat16)
    ranked = jnp.dot(mine.astype(jnp.bfloat16), earlier, preferred_element_type=jnp.float32)
    slot_cap = end_count // owners // groups
    slot = my_group * slot_cap + jnp.arange(slot_cap, dtype=jnp.int32)
    matched = mine[:, None, :] & (ranked.astype(jnp.int32)[:, None, :] == slot[None, :, None])
    chosen = jnp.sum(jnp.where(matched, packed[:, None, :], 0), axis=2).reshape(-1)
    ends = chosen.shape[0]
    chosen_live = chosen % 2
    chosen_local = (chosen // 2) % img_dev
    chosen_partner = chosen // (2 * img_dev)
    place = chosen_local[:, None] * patches + jnp.arange(patches, dtype=jnp.int32)[None, :]
    live_rows = jnp.broadcast_to(chosen_live[:, None], (ends, patches)).reshape(1, -1)

    smem = pl.BlockSpec(memory_space=pltpu.SMEM)
    vmem = pl.BlockSpec(memory_space=pltpu.VMEM)
    rows = ends * patches
    totals = pl.pallas_call(
        functools.partial(decode_kernel, HEADS),
        out_shape=jax.ShapeDtypeStruct((wide, own_rows), jnp.float32),
        in_specs=[smem, smem] + [vmem] * 7,
        out_specs=vmem,
        scratch_shapes=[
            pltpu.VMEM((rows, dec_width), jnp.float32),
            pltpu.VMEM((rows, dec_width), jnp.float32),
            pltpu.VMEM((wide, rows), jnp.float32),
        ],
        compiler_params=pltpu.CompilerParams(vmem_limit_bytes=40 * 2**20),
    )(
        chosen_partner, chosen_local, everyone, queries, w_key, value_head, base,
        place.reshape(1, -1), live_rows,
    )
    totals = lax.psum(totals, "grp")
    totals = totals[:channels].reshape(channels, img_dev, patches).transpose(1, 0, 2)
    return join(totals, patches, channels)


def per_device(tokens, w_embed, w_query, *others):
    images = tokens.shape[0] * lax.axis_size("img")
    gathered = images * tokens.shape[1] * w_query.shape[0] * 2
    run = by_owner if gathered <= GATHER_LIMIT else by_executor
    return run(tokens, w_embed, w_query, *others)


def solution(mesh):
    in_specs = (P("img", None, None), P(), P(), P(), P(), P(), P(), P(), P(), P())
    out_specs = (P("img", None), P("img", None))
    return jax.shard_map(
        per_device, mesh=mesh, in_specs=in_specs, out_specs=out_specs, check_vma=False
    )
```

```python
import functools
import math

import jax
import jax.numpy as jnp
from jax import lax
from jax.experimental import pallas as pl
from jax.experimental.pallas import tpu as pltpu
from jax.sharding import PartitionSpec as P

HEADS = 12
PAIR_BLOCK = 8
GATHER_LIMIT = 16 * 2**20
TABLE = 128
LANES = 128


def layer_norm(values):
    center = values - jnp.mean(values, axis=-1, keepdims=True)
    spread = jnp.mean(center * center, axis=-1, keepdims=True)
    return center * lax.rsqrt(spread + 1e-05)


def contribution(head_out):
    confidence = 1.0 + jnp.exp(head_out[..., 3:4, :])
    return jnp.concatenate(
        [confidence * head_out[..., :3, :], confidence, confidence * head_out[..., 4:, :]], axis=-2
    )


def join(totals, patches, channels):
    image_count = totals.shape[0]
    shaped = totals.reshape(image_count, channels, patches)
    confidence = shaped[:, 3:4, :]
    geometry = jnp.concatenate(
        [shaped[:, :3, :] / (1.0 + confidence), jnp.log1p(confidence)], axis=1
    )
    descriptors = shaped[:, 4:, :] / (1.0 + confidence)
    return (
        geometry.reshape(image_count, 4 * patches),
        descriptors.reshape(image_count, (channels - 4) * patches),
    )


def decode_block(embedded, w_query, w_key, w_value, w_out, w_head):
    blocks, side_count, patches, dec_width = embedded.shape
    head_size = dec_width // HEADS
    normed = layer_norm(embedded.astype(jnp.float32)).astype(jnp.bfloat16)

    def project(weight):
        projected = jnp.einsum("bspd,de->bspe", normed, weight, preferred_element_type=jnp.float32)
        return projected.astype(jnp.bfloat16).reshape(blocks, side_count, patches, HEADS, head_size)

    queries = project(w_query)
    key_proj = project(w_key)[:, ::-1]
    value_proj = project(w_value)[:, ::-1]
    scores = jnp.einsum(
        "bsphd,bsqhd->bshpq", queries, key_proj, preferred_element_type=jnp.float32
    ) / math.sqrt(head_size)
    weights = jax.nn.softmax(scores, axis=-1).astype(jnp.bfloat16)
    attended = jnp.einsum(
        "bshpq,bsqhd->bsphd", weights, value_proj, preferred_element_type=jnp.float32
    )
    attended = attended.astype(jnp.bfloat16).reshape(blocks, side_count, patches, dec_width)
    mixed_rows = embedded.astype(jnp.float32) + jnp.einsum(
        "bspd,de->bspe", attended, w_out, preferred_element_type=jnp.float32
    )
    mixed_rows = mixed_rows.astype(jnp.bfloat16)
    head_out = jnp.einsum("bspd,dc->bscp", mixed_rows, w_head, preferred_element_type=jnp.float32)
    return contribution(head_out).reshape(blocks, side_count, -1)


def by_executor(
    tokens, w_embed, w_query, w_key, w_value, w_out, w_head, pair_images, pair_counts, owner_row
):
    img_dev, patches, enc_width = tokens.shape
    channels = w_head.shape[1]
    owners = lax.axis_size("img")
    groups = lax.axis_size("grp")
    pair_cap = pair_images.shape[2]
    slot_cap = max(2, (2 * groups * pair_cap + owners - 1) // owners)
    my_chip = lax.axis_index("img")
    my_group = lax.axis_index("grp")
    end_count = groups * pair_cap * 2
    token_rows = owner_row[pair_images].reshape(owners, end_count)
    source_owner = token_rows // img_dev
    local_row = token_rows % img_dev
    end_index = jnp.arange(end_count, dtype=jnp.int32)
    earlier = end_index[None, :] < end_index[:, None]
    same_owner = source_owner[:, :, None] == source_owner[:, None, :]
    ranked = jnp.sum((same_owner & earlier[None]).astype(jnp.int32), axis=2)
    is_live = jnp.arange(pair_cap, dtype=jnp.int32)[None, None, :] < pair_counts[:, :, None]
    group_table = jnp.broadcast_to(jnp.arange(groups, dtype=jnp.int32)[:, None], (groups, pair_cap))
    slot_table = jnp.broadcast_to(
        jnp.arange(pair_cap, dtype=jnp.int32)[None, :], (groups, pair_cap)
    )
    dest_group = jnp.broadcast_to(group_table.reshape(1, -1), (owners, groups * pair_cap))
    dest_slot = jnp.broadcast_to(slot_table.reshape(1, -1), (owners, groups * pair_cap))
    my_share = pair_counts[my_chip, my_group]
    live_end = jnp.repeat(is_live.reshape(owners, -1), 2, axis=1)
    group_end = jnp.repeat(dest_group, 2, axis=1)
    slot_end = jnp.repeat(dest_slot, 2, axis=1)
    side_end = end_index % 2
    to_send = live_end & (group_end == my_group) & (source_owner == my_chip)
    slot_index = jnp.arange(slot_cap, dtype=jnp.int32)
    matched = to_send[:, None, :] & (ranked[:, None, :] == slot_index[None, :, None])
    send_index = jnp.sum(jnp.where(matched, local_row[:, None, :], 0), axis=2)
    send_valid = jnp.any(matched, axis=2)
    mine = live_end[my_chip] & (group_end[my_chip] == my_group)
    pair_index = jnp.arange(pair_cap, dtype=jnp.int32)
    side_index = jnp.arange(2, dtype=jnp.int32)
    wanted = mine[None, None, :] & (slot_end[my_chip][None, None, :] == pair_index[:, None, None])
    wanted = wanted & (side_end[None, None, :] == side_index[None, :, None])
    flat_source = source_owner[my_chip] * slot_cap + ranked[my_chip]
    recv_index = jnp.sum(jnp.where(wanted, flat_source[None, None, :], 0), axis=2)
    recv_valid = jnp.any(wanted, axis=2)
    send_mask = send_valid[:, :, None, None].astype(jnp.bfloat16)
    embedded_own = jnp.dot(
        tokens.reshape(img_dev * patches, enc_width), w_embed, preferred_element_type=jnp.float32
    )
    embedded_own = embedded_own.astype(jnp.bfloat16).reshape(img_dev, patches, -1)
    outgoing = embedded_own[send_index] * send_mask
    received = lax.all_to_all(outgoing, "img", split_axis=0, concat_axis=0, tiled=True)
    pair_views = received.reshape(owners * slot_cap, patches, -1)[recv_index]

    def run_block(index_block, totals):
        first_row = index_block * PAIR_BLOCK
        block_views = lax.dynamic_slice_in_dim(pair_views, first_row, PAIR_BLOCK, 0)
        block_result = decode_block(block_views, w_query, w_key, w_value, w_out, w_head)
        return lax.dynamic_update_slice_in_dim(totals, block_result, first_row, 0)

    block_count = (my_share + PAIR_BLOCK - 1) // PAIR_BLOCK
    results = lax.fori_loop(
        0, block_count, run_block, jnp.zeros((pair_cap, 2, channels * patches), jnp.float32)
    )
    results = results * recv_valid[:, :, None].astype(jnp.float32)
    return_map = (
        jnp.arange(owners * slot_cap, dtype=jnp.int32)[:, None] == recv_index.reshape(1, -1)
    ) & recv_valid.reshape(1, -1)
    outgoing_back = jnp.dot(
        return_map.astype(jnp.float32),
        results.reshape(pair_cap * 2, -1),
        precision=lax.Precision.HIGHEST,
        preferred_element_type=jnp.float32,
    )
    returned = lax.all_to_all(
        outgoing_back.reshape(owners, slot_cap, -1), "img", split_axis=0, concat_axis=0, tiled=True
    )
    owner_map = (
        jnp.arange(img_dev, dtype=jnp.int32)[:, None] == send_index.reshape(1, -1)
    ) & send_valid.reshape(1, -1)
    owner_partial = jnp.dot(
        owner_map.astype(jnp.float32),
        returned.reshape(owners * slot_cap, -1),
        precision=lax.Precision.HIGHEST,
        preferred_element_type=jnp.float32,
    )
    totals = lax.psum(owner_partial, "grp")
    return join(totals, patches, channels)


def split3(values):
    high = values.astype(jnp.bfloat16)
    rest = values - high.astype(jnp.float32)
    middle = rest.astype(jnp.bfloat16)
    low = (rest - middle.astype(jnp.float32)).astype(jnp.bfloat16)
    return jnp.concatenate([high, middle, low], axis=0)


def sum3(values):
    part = values.shape[0] // 3
    return values[:part] + values[part : 2 * part] + values[2 * part :]


NT = (((1,), (1,)), ((), ()))


def decode_kernel(
    heads, source_ref, local_ref, normed_ref, query_ref, key_ref, value_ref, base_ref, place_ref,
    live_ref, out_ref, partner_rows, query_rows, attended
):
    ends = source_ref.shape[0]
    patches, width = normed_ref.shape[1:]
    channels = base_ref.shape[0]
    head_size = width // heads
    rows = ends * patches

    def fetch(end, carry):
        at = pl.ds(pl.multiple_of(end * patches, patches), patches)
        own = pl.ds(pl.multiple_of(local_ref[end] * patches, patches), patches)
        partner_rows[at, :] = normed_ref[source_ref[end]].astype(jnp.float32)
        query_rows[at, :] = query_ref[own, :]
        return carry

    lax.fori_loop(0, ends, fetch, 0, unroll=8)

    chunk = min(256, rows)
    group = LANES
    side = LANES // head_size
    lane = lax.broadcasted_iota(jnp.int32, (group, LANES), 1)
    column = lax.broadcasted_iota(jnp.int32, (patches, side * group), 1)
    column_end = (column % group) // patches

    def one_chunk(index, carry):
        first = pl.multiple_of(index * chunk, chunk)
        partner = partner_rows[pl.ds(first, chunk), :].astype(jnp.bfloat16)
        keys = jnp.dot(partner, key_ref[...], preferred_element_type=jnp.float32)
        keys = keys.astype(jnp.bfloat16)
        values = lax.dot_general(
            value_ref[...], partner, NT, preferred_element_type=jnp.float32
        ).astype(jnp.bfloat16)
        for part in range(chunk // group):
            begin = part * group
            all_weights = []
            all_values = []
            for block in range(width // LANES):
                cols = slice(block * LANES, (block + 1) * LANES)
                asked = query_rows[pl.ds(first + begin, group), cols]
                stacked = jnp.concatenate(
                    [jnp.where(lane // head_size == s, asked, 0.0) for s in range(side)], axis=0
                ).astype(jnp.bfloat16)
                scores = lax.dot_general(
                    keys[begin : begin + group, cols], stacked, NT,
                    preferred_element_type=jnp.float32,
                )
                packed = jnp.zeros((patches, side * group), jnp.float32)
                for end in range(group // patches):
                    packed = jnp.where(
                        column_end == end, scores[end * patches : (end + 1) * patches], packed
                    )
                grown = jnp.exp(packed - jnp.max(packed, axis=0, keepdims=True))
                weights = grown / jnp.sum(grown, axis=0, keepdims=True)
                spread = jnp.concatenate(
                    [jnp.where(column_end == end, weights, 0.0) for end in range(group // patches)],
                    axis=0,
                ).astype(jnp.bfloat16)
                for s in range(side):
                    head = block * side + s
                    all_weights.append(spread[:, s * group : (s + 1) * group])
                    all_values.append(
                        values[head * channels : (head + 1) * channels, begin : begin + group]
                    )
            attended[:, pl.ds(pl.multiple_of(first + begin, group), group)] = jnp.dot(
                jnp.concatenate(all_values, axis=1),
                jnp.concatenate(all_weights, axis=0),
                preferred_element_type=jnp.float32,
            )
        return carry

    lax.fori_loop(0, rows // chunk, one_chunk, 0)

    own_rows = base_ref.shape[1]
    target = lax.broadcasted_iota(jnp.int32, (own_rows, rows), 0)
    owner_map = jnp.where(target == place_ref[...], 1.0, 0.0).astype(jnp.bfloat16)
    base = sum3(jnp.dot(split3(base_ref[...]), owner_map, preferred_element_type=jnp.float32))
    head_out = base + attended[...]
    confidence = 1.0 + jnp.exp(head_out[3:4, :])
    channel = lax.broadcasted_iota(jnp.int32, head_out.shape, 0)
    result = jnp.where(channel == 3, confidence, confidence * head_out)
    result = jnp.where(live_ref[...] > 0, result, 0.0)
    out_ref[...] = sum3(
        lax.dot_general(split3(result), owner_map, NT, preferred_element_type=jnp.float32)
    )


def gather_kernel(
    depth, own_ref, all_ref, place_sem, send_sem, recv_sem, mate_send_sem, mate_recv_sem
):
    share = own_ref.shape[0]
    me = lax.axis_index("img")
    core = lax.axis_index("grp")
    layer = me // 4
    tall = me // 2 % 2
    wide = me % 2
    mesh_ids = pl.DeviceIdType.MESH

    def chip(z, y, x):
        return z * 4 + y * 2 + x

    def slot(unit):
        return all_ref.at[pl.ds((unit * 2 + core) * share, share)]

    def copy(unit, way, target, source=None):
        return pltpu.make_async_remote_copy(
            src_ref=slot(unit) if source is None else source,
            dst_ref=slot(unit),
            send_sem=send_sem.at[way, unit],
            recv_sem=recv_sem.at[unit],
            device_id={"img": target, "grp": core},
            device_id_type=mesh_ids,
        )

    def mate_copy(unit, source=None):
        return pltpu.make_async_remote_copy(
            src_ref=slot(unit) if source is None else source,
            dst_ref=slot(unit),
            send_sem=mate_send_sem.at[unit],
            recv_sem=mate_recv_sem.at[unit],
            device_id={"img": me, "grp": 1 - core},
            device_id_type=mesh_ids,
        )

    across = chip(layer, tall, 1 - wide)
    along = chip(layer, 1 - tall, wide)
    has = {1: layer < depth - 1, -1: layer > 0}

    barrier = pltpu.get_barrier_semaphore()
    for target in (across, along):
        pl.semaphore_signal(
            barrier, inc=1, device_id={"img": target, "grp": core}, device_id_type=mesh_ids
        )
    pl.semaphore_signal(
        barrier, inc=1, device_id={"img": me, "grp": 1 - core}, device_id_type=mesh_ids
    )
    for sign in (1, -1):
        @pl.when(has[sign])
        def _():
            pl.semaphore_signal(
                barrier,
                inc=1,
                device_id={"img": me + 4 * sign, "grp": core},
                device_id_type=mesh_ids,
            )
    pl.semaphore_wait(
        barrier, 3 + has[1].astype(jnp.int32) + has[-1].astype(jnp.int32)
    )

    def run(action):
        def at(distance, sign, body):
            z = layer + sign * distance
            if distance == 0:
                body(z)
            else:
                pl.when((z >= 0) & (z < depth))(lambda: body(z))

        for step in range(depth + 2):
            for sign in (1, -1):
                if step < depth and (step > 0 or sign == 1):
                    def column(z):
                        unit = chip(z, tall, wide)
                        own = own_ref if step == 0 else None
                        if step > 0:
                            action("arrive", lambda: copy(unit, 0, across))
                        for onward in (1, -1):
                            if step == 0 or onward == -sign:
                                @pl.when(has[onward])
                                def _():
                                    action(
                                        "send",
                                        lambda: copy(unit, 0 if onward == 1 else 1, me + 4 * onward, own),
                                    )
                        action("send", lambda: copy(unit, 2, across, own))
                        action("send", lambda: copy(unit, 3, along, own))
                        action("send", lambda: mate_copy(unit, own))

                    at(step, sign, column)
                back = step - 1
                if 0 <= back < depth and (back > 0 or sign == 1):
                    def beside(z):
                        unit = chip(z, tall, 1 - wide)
                        action("arrive", lambda: copy(unit, 0, across))
                        @pl.when(z % 2 == 1)
                        def _():
                            action("send", lambda: copy(unit, 3, along))
                        action("send", lambda: mate_copy(unit))
                        unit_up = chip(z, 1 - tall, wide)
                        action("arrive", lambda: copy(unit_up, 0, across))
                        @pl.when(z % 2 == 0)
                        def _():
                            action("send", lambda: copy(unit_up, 2, across))
                        action("send", lambda: mate_copy(unit_up))

                    at(back, sign, beside)
                back2 = step - 2
                if 0 <= back2 < depth and (back2 > 0 or sign == 1):
                    def opposite(z):
                        unit = chip(z, 1 - tall, 1 - wide)
                        action("arrive", lambda: copy(unit, 0, across))
                        action("send", lambda: mate_copy(unit))

                    at(back2, sign, opposite)

    def begin(kind, descriptor):
        if kind == "send":
            descriptor().start()
        else:
            descriptor().wait_recv()

    def finish(kind, descriptor):
        if kind == "send":
            descriptor().wait_send()

    place = pltpu.make_async_copy(own_ref, slot(me), place_sem)
    place.start()
    run(begin)
    run(finish)
    place.wait()

    def from_mate(unit, carry):
        theirs = all_ref.at[pl.ds((unit * 2 + 1 - core) * share, share)]
        pltpu.make_async_remote_copy(
            src_ref=theirs,
            dst_ref=theirs,
            send_sem=mate_send_sem.at[unit],
            recv_sem=mate_recv_sem.at[unit],
            device_id={"img": me, "grp": 1 - core},
            device_id_type=mesh_ids,
        ).wait_recv()
        return carry

    lax.fori_loop(0, 4 * depth, from_mate, 0)


def gather_rows(outgoing, owners):
    share, patches, width = outgoing.shape
    vmem = pl.BlockSpec(memory_space=pltpu.VMEM)
    return pl.pallas_call(
        functools.partial(gather_kernel, owners // 4),
        out_shape=jax.ShapeDtypeStruct((owners * 2 * share, patches, width), outgoing.dtype),
        in_specs=[vmem],
        out_specs=vmem,
        scratch_shapes=[
            pltpu.SemaphoreType.DMA,
            pltpu.SemaphoreType.DMA((4, owners)),
            pltpu.SemaphoreType.DMA((owners,)),
            pltpu.SemaphoreType.DMA((owners,)),
            pltpu.SemaphoreType.DMA((owners,)),
        ],
        compiler_params=pltpu.CompilerParams(
            collective_id=0, has_side_effects=True, vmem_limit_bytes=24 * 2**20
        ),
    )(outgoing)


def look_up(owner_row, ids, img_dev):
    span = min(TABLE, owner_row.shape[0])
    table = owner_row.reshape(-1, span)
    parts = jnp.concatenate([table // img_dev, table % img_dev], axis=0).astype(jnp.bfloat16)
    hot = ids[None, :] % span == jnp.arange(span, dtype=jnp.int32)[:, None]
    found = jnp.dot(parts, hot.astype(jnp.bfloat16), preferred_element_type=jnp.float32)
    found = found.reshape(2, -1, ids.shape[0])
    pick = jnp.arange(found.shape[1], dtype=jnp.int32)[:, None] == ids[None, :] // span
    found = jnp.sum(jnp.where(pick[None], found, 0.0), axis=1).astype(jnp.int32)
    return found[0], found[1]


def by_owner(
    tokens, w_embed, w_query, w_key, w_value, w_out, w_head, pair_images, pair_counts, owner_row
):
    img_dev, patches, enc_width = tokens.shape
    dec_width, channels = w_head.shape
    owners = lax.axis_size("img")
    groups = lax.axis_size("grp")
    pair_cap = pair_images.shape[2]
    my_chip = lax.axis_index("img")
    my_group = lax.axis_index("grp")
    head_size = dec_width // HEADS
    own_rows = img_dev * patches
    share = img_dev // groups
    embedded = jnp.dot(
        tokens.reshape(own_rows, enc_width), w_embed, preferred_element_type=jnp.float32
    ).astype(jnp.bfloat16)
    normed = layer_norm(embedded.astype(jnp.float32)).astype(jnp.bfloat16)
    outgoing = lax.dynamic_slice_in_dim(
        normed.reshape(img_dev, patches, dec_width), my_group * share, share, 0
    )
    everyone = gather_rows(outgoing, owners)

    queries = jnp.dot(normed, w_query, preferred_element_type=jnp.float32)
    queries = queries.astype(jnp.bfloat16).astype(jnp.float32) / math.sqrt(head_size)
    wide = -(-channels // 8) * 8
    head_weight = jnp.pad(w_head, ((0, 0), (0, wide - channels)))
    base = lax.dot_general(
        head_weight, embedded, (((0,), (1,)), ((), ())), preferred_element_type=jnp.float32
    )
    out_head = jnp.dot(w_out, head_weight, preferred_element_type=jnp.float32)
    value_head = jnp.einsum(
        "hdc,ihd->hci",
        out_head.reshape(HEADS, head_size, wide),
        w_value.astype(jnp.float32).reshape(dec_width, HEADS, head_size),
        precision=lax.Precision.HIGHEST,
        preferred_element_type=jnp.float32,
    )
    value_head = value_head.reshape(HEADS * wide, dec_width).astype(jnp.bfloat16)

    end_count = groups * pair_cap * 2
    sides = [pair_images[..., s].reshape(owners, groups * pair_cap) for s in range(2)]
    ids = jnp.concatenate(sides, axis=1)
    owner, local = look_up(owner_row, ids.reshape(-1), img_dev)
    owner = owner.reshape(owners, end_count)
    local = local.reshape(owners, end_count)
    image_row = owner * img_dev + local
    half = end_count // 2
    partner = jnp.concatenate([image_row[:, half:], image_row[:, :half]], axis=1)
    live = jnp.arange(pair_cap, dtype=jnp.int32)[None, None, :] < pair_counts[:, :, None]
    live = live.reshape(owners, half).astype(jnp.int32)
    live = jnp.concatenate([live, live], axis=1)
    packed = (partner * img_dev + local) * 2 + live
    mine = owner == my_chip
    end_index = jnp.arange(end_count, dtype=jnp.int32)
    earlier = (end_index[:, None] < end_index[None, :]).astype(jnp.bfloat16)
    ranked = jnp.dot(mine.astype(jnp.bfloat16), earlier, preferred_element_type=jnp.float32)
    slot_cap = end_count // owners // groups
    slot = my_group * slot_cap + jnp.arange(slot_cap, dtype=jnp.int32)
    matched = mine[:, None, :] & (ranked.astype(jnp.int32)[:, None, :] == slot[None, :, None])
    chosen = jnp.sum(jnp.where(matched, packed[:, None, :], 0), axis=2).reshape(-1)
    ends = chosen.shape[0]
    chosen_live = chosen % 2
    chosen_local = (chosen // 2) % img_dev
    chosen_partner = chosen // (2 * img_dev)
    place = chosen_local[:, None] * patches + jnp.arange(patches, dtype=jnp.int32)[None, :]
    live_rows = jnp.broadcast_to(chosen_live[:, None], (ends, patches)).reshape(1, -1)

    smem = pl.BlockSpec(memory_space=pltpu.SMEM)
    vmem = pl.BlockSpec(memory_space=pltpu.VMEM)
    rows = ends * patches
    totals = pl.pallas_call(
        functools.partial(decode_kernel, HEADS),
        out_shape=jax.ShapeDtypeStruct((wide, own_rows), jnp.float32),
        in_specs=[smem, smem] + [vmem] * 7,
        out_specs=vmem,
        scratch_shapes=[
            pltpu.VMEM((rows, dec_width), jnp.float32),
            pltpu.VMEM((rows, dec_width), jnp.float32),
            pltpu.VMEM((wide, rows), jnp.float32),
        ],
        compiler_params=pltpu.CompilerParams(vmem_limit_bytes=40 * 2**20),
    )(
        chosen_partner, chosen_local, everyone, queries, w_key, value_head, base,
        place.reshape(1, -1), live_rows,
    )
    totals = lax.psum(totals, "grp")
    totals = totals[:channels].reshape(channels, img_dev, patches).transpose(1, 0, 2)
    return join(totals, patches, channels)


def per_device(tokens, w_embed, w_query, *others):
    images = tokens.shape[0] * lax.axis_size("img")
    gathered = images * tokens.shape[1] * w_query.shape[0] * 2
    run = by_owner if gathered <= GATHER_LIMIT else by_executor
    return run(tokens, w_embed, w_query, *others)


def solution(mesh):
    in_specs = (P("img", None, None), P(), P(), P(), P(), P(), P(), P(), P(), P())
    out_specs = (P("img", None), P("img", None))
    return jax.shard_map(
        per_device, mesh=mesh, in_specs=in_specs, out_specs=out_specs, check_vma=False
    )
```

```python
import functools
import math

import jax
import jax.numpy as jnp
from jax import lax
from jax.experimental import pallas as pl
from jax.experimental.pallas import tpu as pltpu
from jax.sharding import PartitionSpec as P

HEADS = 12
PAIR_BLOCK = 8
GATHER_LIMIT = 16 * 2**20
TABLE = 128
LANES = 128


def layer_norm(values):
    center = values - jnp.mean(values, axis=-1, keepdims=True)
    spread = jnp.mean(center * center, axis=-1, keepdims=True)
    return center * lax.rsqrt(spread + 1e-05)


def contribution(head_out):
    confidence = 1.0 + jnp.exp(head_out[..., 3:4, :])
    return jnp.concatenate(
        [confidence * head_out[..., :3, :], confidence, confidence * head_out[..., 4:, :]], axis=-2
    )


def join(totals, patches, channels):
    image_count = totals.shape[0]
    shaped = totals.reshape(image_count, channels, patches)
    confidence = shaped[:, 3:4, :]
    geometry = jnp.concatenate(
        [shaped[:, :3, :] / (1.0 + confidence), jnp.log1p(confidence)], axis=1
    )
    descriptors = shaped[:, 4:, :] / (1.0 + confidence)
    return (
        geometry.reshape(image_count, 4 * patches),
        descriptors.reshape(image_count, (channels - 4) * patches),
    )


def decode_block(embedded, w_query, w_key, w_value, w_out, w_head):
    blocks, side_count, patches, dec_width = embedded.shape
    head_size = dec_width // HEADS
    normed = layer_norm(embedded.astype(jnp.float32)).astype(jnp.bfloat16)

    def project(weight):
        projected = jnp.einsum("bspd,de->bspe", normed, weight, preferred_element_type=jnp.float32)
        return projected.astype(jnp.bfloat16).reshape(blocks, side_count, patches, HEADS, head_size)

    queries = project(w_query)
    key_proj = project(w_key)[:, ::-1]
    value_proj = project(w_value)[:, ::-1]
    scores = jnp.einsum(
        "bsphd,bsqhd->bshpq", queries, key_proj, preferred_element_type=jnp.float32
    ) / math.sqrt(head_size)
    weights = jax.nn.softmax(scores, axis=-1).astype(jnp.bfloat16)
    attended = jnp.einsum(
        "bshpq,bsqhd->bsphd", weights, value_proj, preferred_element_type=jnp.float32
    )
    attended = attended.astype(jnp.bfloat16).reshape(blocks, side_count, patches, dec_width)
    mixed_rows = embedded.astype(jnp.float32) + jnp.einsum(
        "bspd,de->bspe", attended, w_out, preferred_element_type=jnp.float32
    )
    mixed_rows = mixed_rows.astype(jnp.bfloat16)
    head_out = jnp.einsum("bspd,dc->bscp", mixed_rows, w_head, preferred_element_type=jnp.float32)
    return contribution(head_out).reshape(blocks, side_count, -1)


def by_executor(
    tokens, w_embed, w_query, w_key, w_value, w_out, w_head, pair_images, pair_counts, owner_row
):
    img_dev, patches, enc_width = tokens.shape
    channels = w_head.shape[1]
    owners = lax.axis_size("img")
    groups = lax.axis_size("grp")
    pair_cap = pair_images.shape[2]
    slot_cap = max(2, (2 * groups * pair_cap + owners - 1) // owners)
    my_chip = lax.axis_index("img")
    my_group = lax.axis_index("grp")
    end_count = groups * pair_cap * 2
    token_rows = owner_row[pair_images].reshape(owners, end_count)
    source_owner = token_rows // img_dev
    local_row = token_rows % img_dev
    end_index = jnp.arange(end_count, dtype=jnp.int32)
    earlier = end_index[None, :] < end_index[:, None]
    same_owner = source_owner[:, :, None] == source_owner[:, None, :]
    ranked = jnp.sum((same_owner & earlier[None]).astype(jnp.int32), axis=2)
    is_live = jnp.arange(pair_cap, dtype=jnp.int32)[None, None, :] < pair_counts[:, :, None]
    group_table = jnp.broadcast_to(jnp.arange(groups, dtype=jnp.int32)[:, None], (groups, pair_cap))
    slot_table = jnp.broadcast_to(
        jnp.arange(pair_cap, dtype=jnp.int32)[None, :], (groups, pair_cap)
    )
    dest_group = jnp.broadcast_to(group_table.reshape(1, -1), (owners, groups * pair_cap))
    dest_slot = jnp.broadcast_to(slot_table.reshape(1, -1), (owners, groups * pair_cap))
    my_share = pair_counts[my_chip, my_group]
    live_end = jnp.repeat(is_live.reshape(owners, -1), 2, axis=1)
    group_end = jnp.repeat(dest_group, 2, axis=1)
    slot_end = jnp.repeat(dest_slot, 2, axis=1)
    side_end = end_index % 2
    to_send = live_end & (group_end == my_group) & (source_owner == my_chip)
    slot_index = jnp.arange(slot_cap, dtype=jnp.int32)
    matched = to_send[:, None, :] & (ranked[:, None, :] == slot_index[None, :, None])
    send_index = jnp.sum(jnp.where(matched, local_row[:, None, :], 0), axis=2)
    send_valid = jnp.any(matched, axis=2)
    mine = live_end[my_chip] & (group_end[my_chip] == my_group)
    pair_index = jnp.arange(pair_cap, dtype=jnp.int32)
    side_index = jnp.arange(2, dtype=jnp.int32)
    wanted = mine[None, None, :] & (slot_end[my_chip][None, None, :] == pair_index[:, None, None])
    wanted = wanted & (side_end[None, None, :] == side_index[None, :, None])
    flat_source = source_owner[my_chip] * slot_cap + ranked[my_chip]
    recv_index = jnp.sum(jnp.where(wanted, flat_source[None, None, :], 0), axis=2)
    recv_valid = jnp.any(wanted, axis=2)
    send_mask = send_valid[:, :, None, None].astype(jnp.bfloat16)
    embedded_own = jnp.dot(
        tokens.reshape(img_dev * patches, enc_width), w_embed, preferred_element_type=jnp.float32
    )
    embedded_own = embedded_own.astype(jnp.bfloat16).reshape(img_dev, patches, -1)
    outgoing = embedded_own[send_index] * send_mask
    received = lax.all_to_all(outgoing, "img", split_axis=0, concat_axis=0, tiled=True)
    pair_views = received.reshape(owners * slot_cap, patches, -1)[recv_index]

    def run_block(index_block, totals):
        first_row = index_block * PAIR_BLOCK
        block_views = lax.dynamic_slice_in_dim(pair_views, first_row, PAIR_BLOCK, 0)
        block_result = decode_block(block_views, w_query, w_key, w_value, w_out, w_head)
        return lax.dynamic_update_slice_in_dim(totals, block_result, first_row, 0)

    block_count = (my_share + PAIR_BLOCK - 1) // PAIR_BLOCK
    results = lax.fori_loop(
        0, block_count, run_block, jnp.zeros((pair_cap, 2, channels * patches), jnp.float32)
    )
    results = results * recv_valid[:, :, None].astype(jnp.float32)
    return_map = (
        jnp.arange(owners * slot_cap, dtype=jnp.int32)[:, None] == recv_index.reshape(1, -1)
    ) & recv_valid.reshape(1, -1)
    outgoing_back = jnp.dot(
        return_map.astype(jnp.float32),
        results.reshape(pair_cap * 2, -1),
        precision=lax.Precision.HIGHEST,
        preferred_element_type=jnp.float32,
    )
    returned = lax.all_to_all(
        outgoing_back.reshape(owners, slot_cap, -1), "img", split_axis=0, concat_axis=0, tiled=True
    )
    owner_map = (
        jnp.arange(img_dev, dtype=jnp.int32)[:, None] == send_index.reshape(1, -1)
    ) & send_valid.reshape(1, -1)
    owner_partial = jnp.dot(
        owner_map.astype(jnp.float32),
        returned.reshape(owners * slot_cap, -1),
        precision=lax.Precision.HIGHEST,
        preferred_element_type=jnp.float32,
    )
    totals = lax.psum(owner_partial, "grp")
    return join(totals, patches, channels)


def split3(values):
    high = values.astype(jnp.bfloat16)
    rest = values - high.astype(jnp.float32)
    middle = rest.astype(jnp.bfloat16)
    low = (rest - middle.astype(jnp.float32)).astype(jnp.bfloat16)
    return jnp.concatenate([high, middle, low], axis=0)


def sum3(values):
    part = values.shape[0] // 3
    return values[:part] + values[part : 2 * part] + values[2 * part :]


NT = (((1,), (1,)), ((), ()))


def decode_kernel(
    heads, source_ref, local_ref, normed_ref, query_ref, key_ref, value_ref, base_ref, place_ref,
    live_ref, out_ref, partner_rows, query_rows, attended
):
    ends = source_ref.shape[0]
    patches, width = normed_ref.shape[1:]
    channels = base_ref.shape[0]
    head_size = width // heads
    rows = ends * patches

    def fetch(end, carry):
        at = pl.ds(pl.multiple_of(end * patches, patches), patches)
        own = pl.ds(pl.multiple_of(local_ref[end] * patches, patches), patches)
        partner_rows[at, :] = normed_ref[source_ref[end]].astype(jnp.float32)
        query_rows[at, :] = query_ref[own, :]
        return carry

    lax.fori_loop(0, ends, fetch, 0, unroll=8)

    chunk = min(256, rows)
    group = LANES
    side = LANES // head_size
    lane = lax.broadcasted_iota(jnp.int32, (group, LANES), 1)
    column = lax.broadcasted_iota(jnp.int32, (patches, side * group), 1)
    column_end = (column % group) // patches

    def one_chunk(index, carry):
        first = pl.multiple_of(index * chunk, chunk)
        partner = partner_rows[pl.ds(first, chunk), :].astype(jnp.bfloat16)
        keys = jnp.dot(partner, key_ref[...], preferred_element_type=jnp.float32)
        keys = keys.astype(jnp.bfloat16)
        values = lax.dot_general(
            value_ref[...], partner, NT, preferred_element_type=jnp.float32
        ).astype(jnp.bfloat16)
        for part in range(chunk // group):
            begin = part * group
            all_weights = []
            all_values = []
            for block in range(width // LANES):
                cols = slice(block * LANES, (block + 1) * LANES)
                asked = query_rows[pl.ds(first + begin, group), cols]
                stacked = jnp.concatenate(
                    [jnp.where(lane // head_size == s, asked, 0.0) for s in range(side)], axis=0
                ).astype(jnp.bfloat16)
                scores = lax.dot_general(
                    keys[begin : begin + group, cols], stacked, NT,
                    preferred_element_type=jnp.float32,
                )
                packed = jnp.zeros((patches, side * group), jnp.float32)
                for end in range(group // patches):
                    packed = jnp.where(
                        column_end == end, scores[end * patches : (end + 1) * patches], packed
                    )
                grown = jnp.exp(packed - jnp.max(packed, axis=0, keepdims=True))
                weights = grown / jnp.sum(grown, axis=0, keepdims=True)
                spread = jnp.concatenate(
                    [jnp.where(column_end == end, weights, 0.0) for end in range(group // patches)],
                    axis=0,
                ).astype(jnp.bfloat16)
                for s in range(side):
                    head = block * side + s
                    all_weights.append(spread[:, s * group : (s + 1) * group])
                    all_values.append(
                        values[head * channels : (head + 1) * channels, begin : begin + group]
                    )
            attended[:, pl.ds(pl.multiple_of(first + begin, group), group)] = jnp.dot(
                jnp.concatenate(all_values, axis=1),
                jnp.concatenate(all_weights, axis=0),
                preferred_element_type=jnp.float32,
            )
        return carry

    lax.fori_loop(0, rows // chunk, one_chunk, 0)

    own_rows = base_ref.shape[1]
    target = lax.broadcasted_iota(jnp.int32, (own_rows, rows), 0)
    owner_map = jnp.where(target == place_ref[...], 1.0, 0.0).astype(jnp.bfloat16)
    base = sum3(jnp.dot(split3(base_ref[...]), owner_map, preferred_element_type=jnp.float32))
    head_out = base + attended[...]
    confidence = 1.0 + jnp.exp(head_out[3:4, :])
    channel = lax.broadcasted_iota(jnp.int32, head_out.shape, 0)
    result = jnp.where(channel == 3, confidence, confidence * head_out)
    result = jnp.where(live_ref[...] > 0, result, 0.0)
    out_ref[...] = sum3(
        lax.dot_general(split3(result), owner_map, NT, preferred_element_type=jnp.float32)
    )


def gather_kernel(
    depth, heads, own_ref, normed_ref, embedded_ref, head_ref, query_hbm, out_hbm, value_hbm,
    all_ref, query_ref, value_ref, base_ref, weights, weight_sem, place_sem, send_sem, recv_sem,
    mate_send_sem, mate_recv_sem
):
    share = own_ref.shape[0]
    me = lax.axis_index("img")
    core = lax.axis_index("grp")
    layer = me // 4
    tall = me // 2 % 2
    wide = me % 2
    mesh_ids = pl.DeviceIdType.MESH
    loads = [
        pltpu.make_async_copy(source, weights.at[index], weight_sem.at[index])
        for index, source in enumerate((query_hbm, out_hbm, value_hbm))
    ]
    for load in loads:
        load.start()

    def own_queries():
        head_size = normed_ref.shape[1] // heads
        loads[0].wait()
        asked = jnp.dot(normed_ref[...], weights[0], preferred_element_type=jnp.float32)
        query_ref[...] = asked.astype(jnp.bfloat16).astype(jnp.float32) / math.sqrt(head_size)
        base_ref[...] = lax.dot_general(
            head_ref[...], embedded_ref[...], NT, preferred_element_type=jnp.float32
        )

    def value_to_head():
        head_size = normed_ref.shape[1] // heads
        channels = head_ref.shape[0]
        loads[1].wait()
        out_head = lax.dot_general(
            head_ref[...], weights[1], NT, preferred_element_type=jnp.float32
        )
        tiled = jnp.concatenate([out_head] * heads, axis=0)
        row = lax.broadcasted_iota(jnp.int32, tiled.shape, 0)
        column = lax.broadcasted_iota(jnp.int32, tiled.shape, 1)
        tiled = jnp.where(row // channels == column // head_size, tiled, 0.0)
        high = tiled.astype(jnp.bfloat16)
        low = (tiled - high.astype(jnp.float32)).astype(jnp.bfloat16)
        loads[2].wait()
        value_ref[...] = (
            lax.dot_general(high, weights[2], NT, preferred_element_type=jnp.float32)
            + lax.dot_general(low, weights[2], NT, preferred_element_type=jnp.float32)
        ).astype(jnp.bfloat16)

    def chip(z, y, x):
        return z * 4 + y * 2 + x

    def slot(unit):
        return all_ref.at[pl.ds((unit * 2 + core) * share, share)]

    def copy(unit, way, target, source=None):
        return pltpu.make_async_remote_copy(
            src_ref=slot(unit) if source is None else source,
            dst_ref=slot(unit),
            send_sem=send_sem.at[way, unit],
            recv_sem=recv_sem.at[unit],
            device_id={"img": target, "grp": core},
            device_id_type=mesh_ids,
        )

    def mate_copy(unit, source=None):
        return pltpu.make_async_remote_copy(
            src_ref=slot(unit) if source is None else source,
            dst_ref=slot(unit),
            send_sem=mate_send_sem.at[unit],
            recv_sem=mate_recv_sem.at[unit],
            device_id={"img": me, "grp": 1 - core},
            device_id_type=mesh_ids,
        )

    across = chip(layer, tall, 1 - wide)
    along = chip(layer, 1 - tall, wide)
    has = {1: layer < depth - 1, -1: layer > 0}

    barrier = pltpu.get_barrier_semaphore()
    for target in (across, along):
        pl.semaphore_signal(
            barrier, inc=1, device_id={"img": target, "grp": core}, device_id_type=mesh_ids
        )
    pl.semaphore_signal(
        barrier, inc=1, device_id={"img": me, "grp": 1 - core}, device_id_type=mesh_ids
    )
    for sign in (1, -1):
        @pl.when(has[sign])
        def _():
            pl.semaphore_signal(
                barrier,
                inc=1,
                device_id={"img": me + 4 * sign, "grp": core},
                device_id_type=mesh_ids,
            )
    pl.semaphore_wait(
        barrier, 3 + has[1].astype(jnp.int32) + has[-1].astype(jnp.int32)
    )

    def run(action, between):
        def at(distance, sign, body):
            z = layer + sign * distance
            if distance == 0:
                body(z)
            else:
                pl.when((z >= 0) & (z < depth))(lambda: body(z))

        for step in range(depth + 2):
            for sign in (1, -1):
                if step < depth and (step > 0 or sign == 1):
                    def column(z):
                        unit = chip(z, tall, wide)
                        own = own_ref if step == 0 else None
                        if step > 0:
                            action("arrive", lambda: copy(unit, 0, across))
                        for onward in (1, -1):
                            if step == 0 or onward == -sign:
                                @pl.when(has[onward])
                                def _():
                                    action(
                                        "send",
                                        lambda: copy(unit, 0 if onward == 1 else 1, me + 4 * onward, own),
                                    )
                        action("send", lambda: copy(unit, 2, across, own))
                        action("send", lambda: copy(unit, 3, along, own))
                        action("send", lambda: mate_copy(unit, own))

                    at(step, sign, column)
                back = step - 1
                if 0 <= back < depth and (back > 0 or sign == 1):
                    def beside(z):
                        unit = chip(z, tall, 1 - wide)
                        action("arrive", lambda: copy(unit, 0, across))
                        @pl.when(z % 2 == 1)
                        def _():
                            action("send", lambda: copy(unit, 3, along))
                        action("send", lambda: mate_copy(unit))
                        unit_up = chip(z, 1 - tall, wide)
                        action("arrive", lambda: copy(unit_up, 0, across))
                        @pl.when(z % 2 == 0)
                        def _():
                            action("send", lambda: copy(unit_up, 2, across))
                        action("send", lambda: mate_copy(unit_up))

                    at(back, sign, beside)
                back2 = step - 2
                if 0 <= back2 < depth and (back2 > 0 or sign == 1):
                    def opposite(z):
                        unit = chip(z, 1 - tall, 1 - wide)
                        action("arrive", lambda: copy(unit, 0, across))
                        action("send", lambda: mate_copy(unit))

                    at(back2, sign, opposite)
            if step in between:
                between[step]()

    def begin(kind, descriptor):
        if kind == "send":
            descriptor().start()
        else:
            descriptor().wait_recv()

    def finish(kind, descriptor):
        if kind == "send":
            descriptor().wait_send()

    place = pltpu.make_async_copy(own_ref, slot(me), place_sem)
    place.start()
    run(begin, {0: own_queries, 1: value_to_head})
    run(finish, {})
    place.wait()

    def from_mate(unit, carry):
        theirs = all_ref.at[pl.ds((unit * 2 + 1 - core) * share, share)]
        pltpu.make_async_remote_copy(
            src_ref=theirs,
            dst_ref=theirs,
            send_sem=mate_send_sem.at[unit],
            recv_sem=mate_recv_sem.at[unit],
            device_id={"img": me, "grp": 1 - core},
            device_id_type=mesh_ids,
        ).wait_recv()
        return carry

    lax.fori_loop(0, 4 * depth, from_mate, 0)


def gather_rows(outgoing, owners, normed, embedded, head_weight, w_query, w_out, w_value):
    share, patches, width = outgoing.shape
    wide = head_weight.shape[0]
    vmem = pl.BlockSpec(memory_space=pltpu.VMEM)
    away = pl.BlockSpec(memory_space=pl.ANY)
    return pl.pallas_call(
        functools.partial(gather_kernel, owners // 4, HEADS),
        out_shape=(
            jax.ShapeDtypeStruct((owners * 2 * share, patches, width), outgoing.dtype),
            jax.ShapeDtypeStruct(normed.shape, jnp.float32),
            jax.ShapeDtypeStruct((HEADS * wide, width), jnp.bfloat16),
            jax.ShapeDtypeStruct((wide, normed.shape[0]), jnp.float32),
        ),
        in_specs=[vmem] * 4 + [away] * 3,
        out_specs=(vmem,) * 4,
        scratch_shapes=[
            pltpu.VMEM((3, width, width), jnp.bfloat16),
            pltpu.SemaphoreType.DMA((3,)),
            pltpu.SemaphoreType.DMA,
            pltpu.SemaphoreType.DMA((4, owners)),
            pltpu.SemaphoreType.DMA((owners,)),
            pltpu.SemaphoreType.DMA((owners,)),
            pltpu.SemaphoreType.DMA((owners,)),
        ],
        compiler_params=pltpu.CompilerParams(
            collective_id=0, has_side_effects=True, vmem_limit_bytes=32 * 2**20
        ),
    )(outgoing, normed, embedded, head_weight, w_query, w_out, w_value)


def look_up(owner_row, ids, img_dev):
    span = min(TABLE, owner_row.shape[0])
    table = owner_row.reshape(-1, span)
    parts = jnp.concatenate([table // img_dev, table % img_dev], axis=0).astype(jnp.bfloat16)
    hot = ids[None, :] % span == jnp.arange(span, dtype=jnp.int32)[:, None]
    found = jnp.dot(parts, hot.astype(jnp.bfloat16), preferred_element_type=jnp.float32)
    found = found.reshape(2, -1, ids.shape[0])
    pick = jnp.arange(found.shape[1], dtype=jnp.int32)[:, None] == ids[None, :] // span
    found = jnp.sum(jnp.where(pick[None], found, 0.0), axis=1).astype(jnp.int32)
    return found[0], found[1]


def by_owner(
    tokens, w_embed, w_query, w_key, w_value, w_out, w_head, pair_images, pair_counts, owner_row
):
    img_dev, patches, enc_width = tokens.shape
    dec_width, channels = w_head.shape
    owners = lax.axis_size("img")
    groups = lax.axis_size("grp")
    pair_cap = pair_images.shape[2]
    my_chip = lax.axis_index("img")
    my_group = lax.axis_index("grp")
    own_rows = img_dev * patches
    share = img_dev // groups
    embedded = jnp.dot(
        tokens.reshape(own_rows, enc_width), w_embed, preferred_element_type=jnp.float32
    ).astype(jnp.bfloat16)
    normed = layer_norm(embedded.astype(jnp.float32)).astype(jnp.bfloat16)
    outgoing = lax.dynamic_slice_in_dim(
        normed.reshape(img_dev, patches, dec_width), my_group * share, share, 0
    )
    wide = -(-channels // 8) * 8
    head_weight = jnp.pad(w_head.T, ((0, wide - channels), (0, 0)))
    everyone, queries, value_head, base = gather_rows(
        outgoing, owners, normed, embedded, head_weight, w_query, w_out, w_value
    )

    end_count = groups * pair_cap * 2
    sides = [pair_images[..., s].reshape(owners, groups * pair_cap) for s in range(2)]
    ids = jnp.concatenate(sides, axis=1)
    owner, local = look_up(owner_row, ids.reshape(-1), img_dev)
    owner = owner.reshape(owners, end_count)
    local = local.reshape(owners, end_count)
    image_row = owner * img_dev + local
    half = end_count // 2
    partner = jnp.concatenate([image_row[:, half:], image_row[:, :half]], axis=1)
    live = jnp.arange(pair_cap, dtype=jnp.int32)[None, None, :] < pair_counts[:, :, None]
    live = live.reshape(owners, half).astype(jnp.int32)
    live = jnp.concatenate([live, live], axis=1)
    packed = (partner * img_dev + local) * 2 + live
    mine = owner == my_chip
    end_index = jnp.arange(end_count, dtype=jnp.int32)
    earlier = (end_index[:, None] < end_index[None, :]).astype(jnp.bfloat16)
    ranked = jnp.dot(mine.astype(jnp.bfloat16), earlier, preferred_element_type=jnp.float32)
    slot_cap = end_count // owners // groups
    slot = my_group * slot_cap + jnp.arange(slot_cap, dtype=jnp.int32)
    matched = mine[:, None, :] & (ranked.astype(jnp.int32)[:, None, :] == slot[None, :, None])
    chosen = jnp.sum(jnp.where(matched, packed[:, None, :], 0), axis=2).reshape(-1)
    ends = chosen.shape[0]
    chosen_live = chosen % 2
    chosen_local = (chosen // 2) % img_dev
    chosen_partner = chosen // (2 * img_dev)
    place = chosen_local[:, None] * patches + jnp.arange(patches, dtype=jnp.int32)[None, :]
    live_rows = jnp.broadcast_to(chosen_live[:, None], (ends, patches)).reshape(1, -1)

    smem = pl.BlockSpec(memory_space=pltpu.SMEM)
    vmem = pl.BlockSpec(memory_space=pltpu.VMEM)
    rows = ends * patches
    totals = pl.pallas_call(
        functools.partial(decode_kernel, HEADS),
        out_shape=jax.ShapeDtypeStruct((wide, own_rows), jnp.float32),
        in_specs=[smem, smem] + [vmem] * 7,
        out_specs=vmem,
        scratch_shapes=[
            pltpu.VMEM((rows, dec_width), jnp.float32),
            pltpu.VMEM((rows, dec_width), jnp.float32),
            pltpu.VMEM((wide, rows), jnp.float32),
        ],
        compiler_params=pltpu.CompilerParams(vmem_limit_bytes=40 * 2**20),
    )(
        chosen_partner, chosen_local, everyone, queries, w_key, value_head, base,
        place.reshape(1, -1), live_rows,
    )
    totals = lax.psum(totals, "grp")
    totals = totals[:channels].reshape(channels, img_dev, patches).transpose(1, 0, 2)
    return join(totals, patches, channels)


def per_device(tokens, w_embed, w_query, *others):
    images = tokens.shape[0] * lax.axis_size("img")
    gathered = images * tokens.shape[1] * w_query.shape[0] * 2
    run = by_owner if gathered <= GATHER_LIMIT else by_executor
    return run(tokens, w_embed, w_query, *others)


def solution(mesh):
    in_specs = (P("img", None, None), P(), P(), P(), P(), P(), P(), P(), P(), P())
    out_specs = (P("img", None), P("img", None))
    return jax.shard_map(
        per_device, mesh=mesh, in_specs=in_specs, out_specs=out_specs, check_vma=False
    )
```

```python
import functools
import math

import jax
import jax.numpy as jnp
from jax import lax
from jax.experimental import pallas as pl
from jax.experimental.pallas import tpu as pltpu
from jax.sharding import PartitionSpec as P

HEADS = 12
PAIR_BLOCK = 8
GATHER_LIMIT = 16 * 2**20
TABLE = 128
LANES = 128


def layer_norm(values):
    center = values - jnp.mean(values, axis=-1, keepdims=True)
    spread = jnp.mean(center * center, axis=-1, keepdims=True)
    return center * lax.rsqrt(spread + 1e-05)


def contribution(head_out):
    confidence = 1.0 + jnp.exp(head_out[..., 3:4, :])
    return jnp.concatenate(
        [confidence * head_out[..., :3, :], confidence, confidence * head_out[..., 4:, :]], axis=-2
    )


def join(totals, patches, channels):
    image_count = totals.shape[0]
    shaped = totals.reshape(image_count, channels, patches)
    confidence = shaped[:, 3:4, :]
    geometry = jnp.concatenate(
        [shaped[:, :3, :] / (1.0 + confidence), jnp.log1p(confidence)], axis=1
    )
    descriptors = shaped[:, 4:, :] / (1.0 + confidence)
    return (
        geometry.reshape(image_count, 4 * patches),
        descriptors.reshape(image_count, (channels - 4) * patches),
    )


def decode_block(embedded, w_query, w_key, w_value, w_out, w_head):
    blocks, side_count, patches, dec_width = embedded.shape
    head_size = dec_width // HEADS
    normed = layer_norm(embedded.astype(jnp.float32)).astype(jnp.bfloat16)

    def project(weight):
        projected = jnp.einsum("bspd,de->bspe", normed, weight, preferred_element_type=jnp.float32)
        return projected.astype(jnp.bfloat16).reshape(blocks, side_count, patches, HEADS, head_size)

    queries = project(w_query)
    key_proj = project(w_key)[:, ::-1]
    value_proj = project(w_value)[:, ::-1]
    scores = jnp.einsum(
        "bsphd,bsqhd->bshpq", queries, key_proj, preferred_element_type=jnp.float32
    ) / math.sqrt(head_size)
    weights = jax.nn.softmax(scores, axis=-1).astype(jnp.bfloat16)
    attended = jnp.einsum(
        "bshpq,bsqhd->bsphd", weights, value_proj, preferred_element_type=jnp.float32
    )
    attended = attended.astype(jnp.bfloat16).reshape(blocks, side_count, patches, dec_width)
    mixed_rows = embedded.astype(jnp.float32) + jnp.einsum(
        "bspd,de->bspe", attended, w_out, preferred_element_type=jnp.float32
    )
    mixed_rows = mixed_rows.astype(jnp.bfloat16)
    head_out = jnp.einsum("bspd,dc->bscp", mixed_rows, w_head, preferred_element_type=jnp.float32)
    return contribution(head_out).reshape(blocks, side_count, -1)


def by_executor(
    tokens, w_embed, w_query, w_key, w_value, w_out, w_head, pair_images, pair_counts, owner_row
):
    img_dev, patches, enc_width = tokens.shape
    channels = w_head.shape[1]
    owners = lax.axis_size("img")
    groups = lax.axis_size("grp")
    pair_cap = pair_images.shape[2]
    slot_cap = max(2, (2 * groups * pair_cap + owners - 1) // owners)
    my_chip = lax.axis_index("img")
    my_group = lax.axis_index("grp")
    end_count = groups * pair_cap * 2
    token_rows = owner_row[pair_images].reshape(owners, end_count)
    source_owner = token_rows // img_dev
    local_row = token_rows % img_dev
    end_index = jnp.arange(end_count, dtype=jnp.int32)
    earlier = end_index[None, :] < end_index[:, None]
    same_owner = source_owner[:, :, None] == source_owner[:, None, :]
    ranked = jnp.sum((same_owner & earlier[None]).astype(jnp.int32), axis=2)
    is_live = jnp.arange(pair_cap, dtype=jnp.int32)[None, None, :] < pair_counts[:, :, None]
    group_table = jnp.broadcast_to(jnp.arange(groups, dtype=jnp.int32)[:, None], (groups, pair_cap))
    slot_table = jnp.broadcast_to(
        jnp.arange(pair_cap, dtype=jnp.int32)[None, :], (groups, pair_cap)
    )
    dest_group = jnp.broadcast_to(group_table.reshape(1, -1), (owners, groups * pair_cap))
    dest_slot = jnp.broadcast_to(slot_table.reshape(1, -1), (owners, groups * pair_cap))
    my_share = pair_counts[my_chip, my_group]
    live_end = jnp.repeat(is_live.reshape(owners, -1), 2, axis=1)
    group_end = jnp.repeat(dest_group, 2, axis=1)
    slot_end = jnp.repeat(dest_slot, 2, axis=1)
    side_end = end_index % 2
    to_send = live_end & (group_end == my_group) & (source_owner == my_chip)
    slot_index = jnp.arange(slot_cap, dtype=jnp.int32)
    matched = to_send[:, None, :] & (ranked[:, None, :] == slot_index[None, :, None])
    send_index = jnp.sum(jnp.where(matched, local_row[:, None, :], 0), axis=2)
    send_valid = jnp.any(matched, axis=2)
    mine = live_end[my_chip] & (group_end[my_chip] == my_group)
    pair_index = jnp.arange(pair_cap, dtype=jnp.int32)
    side_index = jnp.arange(2, dtype=jnp.int32)
    wanted = mine[None, None, :] & (slot_end[my_chip][None, None, :] == pair_index[:, None, None])
    wanted = wanted & (side_end[None, None, :] == side_index[None, :, None])
    flat_source = source_owner[my_chip] * slot_cap + ranked[my_chip]
    recv_index = jnp.sum(jnp.where(wanted, flat_source[None, None, :], 0), axis=2)
    recv_valid = jnp.any(wanted, axis=2)
    send_mask = send_valid[:, :, None, None].astype(jnp.bfloat16)
    embedded_own = jnp.dot(
        tokens.reshape(img_dev * patches, enc_width), w_embed, preferred_element_type=jnp.float32
    )
    embedded_own = embedded_own.astype(jnp.bfloat16).reshape(img_dev, patches, -1)
    outgoing = embedded_own[send_index] * send_mask
    received = lax.all_to_all(outgoing, "img", split_axis=0, concat_axis=0, tiled=True)
    pair_views = received.reshape(owners * slot_cap, patches, -1)[recv_index]

    def run_block(index_block, totals):
        first_row = index_block * PAIR_BLOCK
        block_views = lax.dynamic_slice_in_dim(pair_views, first_row, PAIR_BLOCK, 0)
        block_result = decode_block(block_views, w_query, w_key, w_value, w_out, w_head)
        return lax.dynamic_update_slice_in_dim(totals, block_result, first_row, 0)

    block_count = (my_share + PAIR_BLOCK - 1) // PAIR_BLOCK
    results = lax.fori_loop(
        0, block_count, run_block, jnp.zeros((pair_cap, 2, channels * patches), jnp.float32)
    )
    results = results * recv_valid[:, :, None].astype(jnp.float32)
    return_map = (
        jnp.arange(owners * slot_cap, dtype=jnp.int32)[:, None] == recv_index.reshape(1, -1)
    ) & recv_valid.reshape(1, -1)
    outgoing_back = jnp.dot(
        return_map.astype(jnp.float32),
        results.reshape(pair_cap * 2, -1),
        precision=lax.Precision.HIGHEST,
        preferred_element_type=jnp.float32,
    )
    returned = lax.all_to_all(
        outgoing_back.reshape(owners, slot_cap, -1), "img", split_axis=0, concat_axis=0, tiled=True
    )
    owner_map = (
        jnp.arange(img_dev, dtype=jnp.int32)[:, None] == send_index.reshape(1, -1)
    ) & send_valid.reshape(1, -1)
    owner_partial = jnp.dot(
        owner_map.astype(jnp.float32),
        returned.reshape(owners * slot_cap, -1),
        precision=lax.Precision.HIGHEST,
        preferred_element_type=jnp.float32,
    )
    totals = lax.psum(owner_partial, "grp")
    return join(totals, patches, channels)


def split3(values):
    high = values.astype(jnp.bfloat16)
    rest = values - high.astype(jnp.float32)
    middle = rest.astype(jnp.bfloat16)
    low = (rest - middle.astype(jnp.float32)).astype(jnp.bfloat16)
    return jnp.concatenate([high, middle, low], axis=0)


def sum3(values):
    part = values.shape[0] // 3
    return values[:part] + values[part : 2 * part] + values[2 * part :]


NT = (((1,), (1,)), ((), ()))


def decode(
    heads, source_ref, local_ref, normed_ref, query_ref, key_ref, value_ref, base_ref, place_ref,
    live_ref, out_ref, partner_rows, query_rows, attended
):
    ends = source_ref.shape[0]
    patches, width = normed_ref.shape[1:]
    channels = base_ref.shape[0]
    head_size = width // heads
    rows = ends * patches

    def fetch(end, carry):
        at = pl.ds(pl.multiple_of(end * patches, patches), patches)
        partner_rows[at, :] = normed_ref[source_ref[end]].astype(jnp.float32)
        query_rows[at, :] = query_ref[local_ref[end]]
        return carry

    lax.fori_loop(0, ends, fetch, 0, unroll=8)

    chunk = min(256, rows)
    group = LANES
    side = LANES // head_size
    lane = lax.broadcasted_iota(jnp.int32, (group, LANES), 1)
    column = lax.broadcasted_iota(jnp.int32, (patches, side * group), 1)
    column_end = (column % group) // patches

    def one_chunk(index, carry):
        first = pl.multiple_of(index * chunk, chunk)
        partner = partner_rows[pl.ds(first, chunk), :].astype(jnp.bfloat16)
        keys = jnp.dot(partner, key_ref[...], preferred_element_type=jnp.float32)
        keys = keys.astype(jnp.bfloat16)
        values = lax.dot_general(
            value_ref[...], partner, NT, preferred_element_type=jnp.float32
        ).astype(jnp.bfloat16)
        for part in range(chunk // group):
            begin = part * group
            all_weights = []
            all_values = []
            for block in range(width // LANES):
                cols = slice(block * LANES, (block + 1) * LANES)
                asked = query_rows[pl.ds(first + begin, group), cols]
                stacked = jnp.concatenate(
                    [jnp.where(lane // head_size == s, asked, 0.0) for s in range(side)], axis=0
                ).astype(jnp.bfloat16)
                scores = lax.dot_general(
                    keys[begin : begin + group, cols], stacked, NT,
                    preferred_element_type=jnp.float32,
                )
                packed = jnp.zeros((patches, side * group), jnp.float32)
                for end in range(group // patches):
                    packed = jnp.where(
                        column_end == end, scores[end * patches : (end + 1) * patches], packed
                    )
                grown = jnp.exp(packed - jnp.max(packed, axis=0, keepdims=True))
                weights = grown / jnp.sum(grown, axis=0, keepdims=True)
                spread = jnp.concatenate(
                    [jnp.where(column_end == end, weights, 0.0) for end in range(group // patches)],
                    axis=0,
                ).astype(jnp.bfloat16)
                for s in range(side):
                    head = block * side + s
                    all_weights.append(spread[:, s * group : (s + 1) * group])
                    all_values.append(
                        values[head * channels : (head + 1) * channels, begin : begin + group]
                    )
            attended[:, pl.ds(pl.multiple_of(first + begin, group), group)] = jnp.dot(
                jnp.concatenate(all_values, axis=1),
                jnp.concatenate(all_weights, axis=0),
                preferred_element_type=jnp.float32,
            )
        return carry

    lax.fori_loop(0, rows // chunk, one_chunk, 0)

    own_rows = base_ref.shape[1]
    target = lax.broadcasted_iota(jnp.int32, (own_rows, rows), 0)
    owner_map = jnp.where(target == place_ref[...], 1.0, 0.0).astype(jnp.bfloat16)
    base = sum3(jnp.dot(split3(base_ref[...]), owner_map, preferred_element_type=jnp.float32))
    head_out = base + attended[...]
    confidence = 1.0 + jnp.exp(head_out[3:4, :])
    channel = lax.broadcasted_iota(jnp.int32, head_out.shape, 0)
    result = jnp.where(channel == 3, confidence, confidence * head_out)
    result = jnp.where(live_ref[...] > 0, result, 0.0)
    out_ref[...] = sum3(
        lax.dot_general(split3(result), owner_map, NT, preferred_element_type=jnp.float32)
    )


def gather_kernel(
    depth, heads, source_ref, local_ref, place_ref, live_ref, own_ref, normed_ref, embedded_ref,
    head_ref, query_hbm, out_hbm, value_hbm, key_hbm, totals_ref, all_ref, query_ref, value_ref,
    base_ref, partner_rows, query_rows, attended, weights, weight_sem, place_sem, send_sem,
    recv_sem, mate_send_sem, mate_recv_sem
):
    share = own_ref.shape[0]
    me = lax.axis_index("img")
    core = lax.axis_index("grp")
    layer = me // 4
    tall = me // 2 % 2
    wide = me % 2
    mesh_ids = pl.DeviceIdType.MESH
    loads = [
        pltpu.make_async_copy(source, weights.at[index], weight_sem.at[index])
        for index, source in enumerate((query_hbm, out_hbm, value_hbm, key_hbm))
    ]
    for load in loads:
        load.start()

    def own_queries():
        head_size = normed_ref.shape[1] // heads
        loads[0].wait()
        asked = jnp.dot(normed_ref[...], weights[0], preferred_element_type=jnp.float32)
        asked = asked.astype(jnp.bfloat16).astype(jnp.float32) / math.sqrt(head_size)
        query_ref[...] = asked.reshape(query_ref.shape)
        base_ref[...] = lax.dot_general(
            head_ref[...], embedded_ref[...], NT, preferred_element_type=jnp.float32
        )

    def value_to_head():
        head_size = normed_ref.shape[1] // heads
        channels = head_ref.shape[0]
        loads[1].wait()
        out_head = lax.dot_general(
            head_ref[...], weights[1], NT, preferred_element_type=jnp.float32
        )
        tiled = jnp.concatenate([out_head] * heads, axis=0)
        row = lax.broadcasted_iota(jnp.int32, tiled.shape, 0)
        column = lax.broadcasted_iota(jnp.int32, tiled.shape, 1)
        tiled = jnp.where(row // channels == column // head_size, tiled, 0.0)
        high = tiled.astype(jnp.bfloat16)
        low = (tiled - high.astype(jnp.float32)).astype(jnp.bfloat16)
        loads[2].wait()
        value_ref[...] = (
            lax.dot_general(high, weights[2], NT, preferred_element_type=jnp.float32)
            + lax.dot_general(low, weights[2], NT, preferred_element_type=jnp.float32)
        ).astype(jnp.bfloat16)

    def chip(z, y, x):
        return z * 4 + y * 2 + x

    def slot(unit):
        return all_ref.at[pl.ds((unit * 2 + core) * share, share)]

    def copy(unit, way, target, source=None):
        return pltpu.make_async_remote_copy(
            src_ref=slot(unit) if source is None else source,
            dst_ref=slot(unit),
            send_sem=send_sem.at[way, unit],
            recv_sem=recv_sem.at[unit],
            device_id={"img": target, "grp": core},
            device_id_type=mesh_ids,
        )

    def mate_copy(unit, source=None):
        return pltpu.make_async_remote_copy(
            src_ref=slot(unit) if source is None else source,
            dst_ref=slot(unit),
            send_sem=mate_send_sem.at[unit],
            recv_sem=mate_recv_sem.at[unit],
            device_id={"img": me, "grp": 1 - core},
            device_id_type=mesh_ids,
        )

    across = chip(layer, tall, 1 - wide)
    along = chip(layer, 1 - tall, wide)
    has = {1: layer < depth - 1, -1: layer > 0}

    barrier = pltpu.get_barrier_semaphore()
    for target in (across, along):
        pl.semaphore_signal(
            barrier, inc=1, device_id={"img": target, "grp": core}, device_id_type=mesh_ids
        )
    pl.semaphore_signal(
        barrier, inc=1, device_id={"img": me, "grp": 1 - core}, device_id_type=mesh_ids
    )
    for sign in (1, -1):
        @pl.when(has[sign])
        def _():
            pl.semaphore_signal(
                barrier,
                inc=1,
                device_id={"img": me + 4 * sign, "grp": core},
                device_id_type=mesh_ids,
            )
    pl.semaphore_wait(
        barrier, 3 + has[1].astype(jnp.int32) + has[-1].astype(jnp.int32)
    )

    def run(action, between):
        def at(distance, sign, body):
            z = layer + sign * distance
            if distance == 0:
                body(z)
            else:
                pl.when((z >= 0) & (z < depth))(lambda: body(z))

        for step in range(depth + 2):
            for sign in (1, -1):
                if step < depth and (step > 0 or sign == 1):
                    def column(z):
                        unit = chip(z, tall, wide)
                        own = own_ref if step == 0 else None
                        if step > 0:
                            action("arrive", lambda: copy(unit, 0, across))
                        for onward in (1, -1):
                            if step == 0 or onward == -sign:
                                @pl.when(has[onward])
                                def _():
                                    action(
                                        "send",
                                        lambda: copy(unit, 0 if onward == 1 else 1, me + 4 * onward, own),
                                    )
                        action("send", lambda: copy(unit, 2, across, own))
                        action("send", lambda: copy(unit, 3, along, own))
                        action("send", lambda: mate_copy(unit, own))

                    at(step, sign, column)
                back = step - 1
                if 0 <= back < depth and (back > 0 or sign == 1):
                    def beside(z):
                        unit = chip(z, tall, 1 - wide)
                        action("arrive", lambda: copy(unit, 0, across))
                        @pl.when(z % 2 == 1)
                        def _():
                            action("send", lambda: copy(unit, 3, along))
                        action("send", lambda: mate_copy(unit))
                        unit_up = chip(z, 1 - tall, wide)
                        action("arrive", lambda: copy(unit_up, 0, across))
                        @pl.when(z % 2 == 0)
                        def _():
                            action("send", lambda: copy(unit_up, 2, across))
                        action("send", lambda: mate_copy(unit_up))

                    at(back, sign, beside)
                back2 = step - 2
                if 0 <= back2 < depth and (back2 > 0 or sign == 1):
                    def opposite(z):
                        unit = chip(z, 1 - tall, 1 - wide)
                        action("arrive", lambda: copy(unit, 0, across))
                        action("send", lambda: mate_copy(unit))

                    at(back2, sign, opposite)
            if step in between:
                between[step]()

    def begin(kind, descriptor):
        if kind == "send":
            descriptor().start()
        else:
            descriptor().wait_recv()

    def finish(kind, descriptor):
        if kind == "send":
            descriptor().wait_send()

    place = pltpu.make_async_copy(own_ref, slot(me), place_sem)
    place.start()
    run(begin, {0: own_queries, 1: value_to_head})
    run(finish, {})
    place.wait()

    def from_mate(unit, carry):
        theirs = all_ref.at[pl.ds((unit * 2 + 1 - core) * share, share)]
        pltpu.make_async_remote_copy(
            src_ref=theirs,
            dst_ref=theirs,
            send_sem=mate_send_sem.at[unit],
            recv_sem=mate_recv_sem.at[unit],
            device_id={"img": me, "grp": 1 - core},
            device_id_type=mesh_ids,
        ).wait_recv()
        return carry

    lax.fori_loop(0, 4 * depth, from_mate, 0)
    loads[3].wait()
    decode(
        heads, source_ref, local_ref, all_ref, query_ref, weights.at[3], value_ref, base_ref,
        place_ref, live_ref, totals_ref, partner_rows, query_rows, attended
    )


def gather_and_decode(
    owners, source, local, place, live_rows, outgoing, normed, embedded, head_weight, w_query,
    w_out, w_value, w_key
):
    share, patches, width = outgoing.shape
    wide = head_weight.shape[0]
    rows = place.shape[1]
    smem = pl.BlockSpec(memory_space=pltpu.SMEM)
    vmem = pl.BlockSpec(memory_space=pltpu.VMEM)
    away = pl.BlockSpec(memory_space=pl.ANY)
    return pl.pallas_call(
        functools.partial(gather_kernel, owners // 4, HEADS),
        out_shape=jax.ShapeDtypeStruct((wide, normed.shape[0]), jnp.float32),
        in_specs=[smem] * 2 + [vmem] * 6 + [away] * 4,
        out_specs=vmem,
        scratch_shapes=[
            pltpu.VMEM((owners * 2 * share, patches, width), outgoing.dtype),
            pltpu.VMEM((normed.shape[0] // patches, patches, width), jnp.float32),
            pltpu.VMEM((HEADS * wide, width), jnp.bfloat16),
            pltpu.VMEM((wide, normed.shape[0]), jnp.float32),
            pltpu.VMEM((rows, width), jnp.float32),
            pltpu.VMEM((rows, width), jnp.float32),
            pltpu.VMEM((wide, rows), jnp.float32),
            pltpu.VMEM((4, width, width), jnp.bfloat16),
            pltpu.SemaphoreType.DMA((4,)),
            pltpu.SemaphoreType.DMA,
            pltpu.SemaphoreType.DMA((4, owners)),
            pltpu.SemaphoreType.DMA((owners,)),
            pltpu.SemaphoreType.DMA((owners,)),
            pltpu.SemaphoreType.DMA((owners,)),
        ],
        compiler_params=pltpu.CompilerParams(
            collective_id=0, has_side_effects=True, vmem_limit_bytes=48 * 2**20
        ),
    )(
        source, local, place, live_rows, outgoing, normed, embedded, head_weight, w_query, w_out,
        w_value, w_key
    )


def look_up(owner_row, ids, img_dev):
    span = min(TABLE, owner_row.shape[0])
    table = owner_row.reshape(-1, span)
    parts = jnp.concatenate([table // img_dev, table % img_dev], axis=0).astype(jnp.bfloat16)
    hot = ids[None, :] % span == jnp.arange(span, dtype=jnp.int32)[:, None]
    found = jnp.dot(parts, hot.astype(jnp.bfloat16), preferred_element_type=jnp.float32)
    found = found.reshape(2, -1, ids.shape[0])
    pick = jnp.arange(found.shape[1], dtype=jnp.int32)[:, None] == ids[None, :] // span
    found = jnp.sum(jnp.where(pick[None], found, 0.0), axis=1).astype(jnp.int32)
    return found[0], found[1]


def by_owner(
    tokens, w_embed, w_query, w_key, w_value, w_out, w_head, pair_images, pair_counts, owner_row
):
    img_dev, patches, enc_width = tokens.shape
    dec_width, channels = w_head.shape
    owners = lax.axis_size("img")
    groups = lax.axis_size("grp")
    pair_cap = pair_images.shape[2]
    my_chip = lax.axis_index("img")
    my_group = lax.axis_index("grp")
    own_rows = img_dev * patches
    share = img_dev // groups
    embedded = jnp.dot(
        tokens.reshape(own_rows, enc_width), w_embed, preferred_element_type=jnp.float32
    ).astype(jnp.bfloat16)
    normed = layer_norm(embedded.astype(jnp.float32)).astype(jnp.bfloat16)
    outgoing = lax.dynamic_slice_in_dim(
        normed.reshape(img_dev, patches, dec_width), my_group * share, share, 0
    )
    wide = -(-channels // 8) * 8
    head_weight = jnp.pad(w_head.T, ((0, wide - channels), (0, 0)))

    end_count = groups * pair_cap * 2
    sides = [pair_images[..., s].reshape(owners, groups * pair_cap) for s in range(2)]
    ids = jnp.concatenate(sides, axis=1)
    owner, local = look_up(owner_row, ids.reshape(-1), img_dev)
    owner = owner.reshape(owners, end_count)
    local = local.reshape(owners, end_count)
    image_row = owner * img_dev + local
    half = end_count // 2
    partner = jnp.concatenate([image_row[:, half:], image_row[:, :half]], axis=1)
    live = jnp.arange(pair_cap, dtype=jnp.int32)[None, None, :] < pair_counts[:, :, None]
    live = live.reshape(owners, half).astype(jnp.int32)
    live = jnp.concatenate([live, live], axis=1)
    packed = (partner * img_dev + local) * 2 + live
    mine = owner == my_chip
    end_index = jnp.arange(end_count, dtype=jnp.int32)
    earlier = (end_index[:, None] < end_index[None, :]).astype(jnp.bfloat16)
    ranked = jnp.dot(mine.astype(jnp.bfloat16), earlier, preferred_element_type=jnp.float32)
    slot_cap = end_count // owners // groups
    slot = my_group * slot_cap + jnp.arange(slot_cap, dtype=jnp.int32)
    matched = mine[:, None, :] & (ranked.astype(jnp.int32)[:, None, :] == slot[None, :, None])
    chosen = jnp.sum(jnp.where(matched, packed[:, None, :], 0), axis=2).reshape(-1)
    ends = chosen.shape[0]
    chosen_live = chosen % 2
    chosen_local = (chosen // 2) % img_dev
    chosen_partner = chosen // (2 * img_dev)
    place = chosen_local[:, None] * patches + jnp.arange(patches, dtype=jnp.int32)[None, :]
    live_rows = jnp.broadcast_to(chosen_live[:, None], (ends, patches)).reshape(1, -1)

    totals = gather_and_decode(
        owners, chosen_partner, chosen_local, place.reshape(1, -1), live_rows, outgoing, normed,
        embedded, head_weight, w_query, w_out, w_value, w_key
    )
    totals = lax.psum(totals, "grp")
    totals = totals[:channels].reshape(channels, img_dev, patches).transpose(1, 0, 2)
    return join(totals, patches, channels)


def per_device(tokens, w_embed, w_query, *others):
    images = tokens.shape[0] * lax.axis_size("img")
    gathered = images * tokens.shape[1] * w_query.shape[0] * 2
    run = by_owner if gathered <= GATHER_LIMIT else by_executor
    return run(tokens, w_embed, w_query, *others)


def solution(mesh):
    in_specs = (P("img", None, None), P(), P(), P(), P(), P(), P(), P(), P(), P())
    out_specs = (P("img", None), P("img", None))
    return jax.shard_map(
        per_device, mesh=mesh, in_specs=in_specs, out_specs=out_specs, check_vma=False
    )
```

```python
import functools
import math

import jax
import jax.numpy as jnp
from jax import lax
from jax.experimental import pallas as pl
from jax.experimental.pallas import tpu as pltpu
from jax.sharding import PartitionSpec as P

HEADS = 12
PAIR_BLOCK = 8
GATHER_LIMIT = 16 * 2**20
TABLE = 128
LANES = 128


def layer_norm(values):
    center = values - jnp.mean(values, axis=-1, keepdims=True)
    spread = jnp.mean(center * center, axis=-1, keepdims=True)
    return center * lax.rsqrt(spread + 1e-05)


def contribution(head_out):
    confidence = 1.0 + jnp.exp(head_out[..., 3:4, :])
    return jnp.concatenate(
        [confidence * head_out[..., :3, :], confidence, confidence * head_out[..., 4:, :]], axis=-2
    )


def join(totals, patches, channels):
    image_count = totals.shape[0]
    shaped = totals.reshape(image_count, channels, patches)
    confidence = shaped[:, 3:4, :]
    geometry = jnp.concatenate(
        [shaped[:, :3, :] / (1.0 + confidence), jnp.log1p(confidence)], axis=1
    )
    descriptors = shaped[:, 4:, :] / (1.0 + confidence)
    return (
        geometry.reshape(image_count, 4 * patches),
        descriptors.reshape(image_count, (channels - 4) * patches),
    )


def decode_block(embedded, w_query, w_key, w_value, w_out, w_head):
    blocks, side_count, patches, dec_width = embedded.shape
    head_size = dec_width // HEADS
    normed = layer_norm(embedded.astype(jnp.float32)).astype(jnp.bfloat16)

    def project(weight):
        projected = jnp.einsum("bspd,de->bspe", normed, weight, preferred_element_type=jnp.float32)
        return projected.astype(jnp.bfloat16).reshape(blocks, side_count, patches, HEADS, head_size)

    queries = project(w_query)
    key_proj = project(w_key)[:, ::-1]
    value_proj = project(w_value)[:, ::-1]
    scores = jnp.einsum(
        "bsphd,bsqhd->bshpq", queries, key_proj, preferred_element_type=jnp.float32
    ) / math.sqrt(head_size)
    weights = jax.nn.softmax(scores, axis=-1).astype(jnp.bfloat16)
    attended = jnp.einsum(
        "bshpq,bsqhd->bsphd", weights, value_proj, preferred_element_type=jnp.float32
    )
    attended = attended.astype(jnp.bfloat16).reshape(blocks, side_count, patches, dec_width)
    mixed_rows = embedded.astype(jnp.float32) + jnp.einsum(
        "bspd,de->bspe", attended, w_out, preferred_element_type=jnp.float32
    )
    mixed_rows = mixed_rows.astype(jnp.bfloat16)
    head_out = jnp.einsum("bspd,dc->bscp", mixed_rows, w_head, preferred_element_type=jnp.float32)
    return contribution(head_out).reshape(blocks, side_count, -1)


def by_executor(
    tokens, w_embed, w_query, w_key, w_value, w_out, w_head, pair_images, pair_counts, owner_row
):
    img_dev, patches, enc_width = tokens.shape
    channels = w_head.shape[1]
    owners = lax.axis_size("img")
    groups = lax.axis_size("grp")
    pair_cap = pair_images.shape[2]
    slot_cap = max(2, (2 * groups * pair_cap + owners - 1) // owners)
    my_chip = lax.axis_index("img")
    my_group = lax.axis_index("grp")
    end_count = groups * pair_cap * 2
    token_rows = owner_row[pair_images].reshape(owners, end_count)
    source_owner = token_rows // img_dev
    local_row = token_rows % img_dev
    end_index = jnp.arange(end_count, dtype=jnp.int32)
    earlier = end_index[None, :] < end_index[:, None]
    same_owner = source_owner[:, :, None] == source_owner[:, None, :]
    ranked = jnp.sum((same_owner & earlier[None]).astype(jnp.int32), axis=2)
    is_live = jnp.arange(pair_cap, dtype=jnp.int32)[None, None, :] < pair_counts[:, :, None]
    group_table = jnp.broadcast_to(jnp.arange(groups, dtype=jnp.int32)[:, None], (groups, pair_cap))
    slot_table = jnp.broadcast_to(
        jnp.arange(pair_cap, dtype=jnp.int32)[None, :], (groups, pair_cap)
    )
    dest_group = jnp.broadcast_to(group_table.reshape(1, -1), (owners, groups * pair_cap))
    dest_slot = jnp.broadcast_to(slot_table.reshape(1, -1), (owners, groups * pair_cap))
    my_share = pair_counts[my_chip, my_group]
    live_end = jnp.repeat(is_live.reshape(owners, -1), 2, axis=1)
    group_end = jnp.repeat(dest_group, 2, axis=1)
    slot_end = jnp.repeat(dest_slot, 2, axis=1)
    side_end = end_index % 2
    to_send = live_end & (group_end == my_group) & (source_owner == my_chip)
    slot_index = jnp.arange(slot_cap, dtype=jnp.int32)
    matched = to_send[:, None, :] & (ranked[:, None, :] == slot_index[None, :, None])
    send_index = jnp.sum(jnp.where(matched, local_row[:, None, :], 0), axis=2)
    send_valid = jnp.any(matched, axis=2)
    mine = live_end[my_chip] & (group_end[my_chip] == my_group)
    pair_index = jnp.arange(pair_cap, dtype=jnp.int32)
    side_index = jnp.arange(2, dtype=jnp.int32)
    wanted = mine[None, None, :] & (slot_end[my_chip][None, None, :] == pair_index[:, None, None])
    wanted = wanted & (side_end[None, None, :] == side_index[None, :, None])
    flat_source = source_owner[my_chip] * slot_cap + ranked[my_chip]
    recv_index = jnp.sum(jnp.where(wanted, flat_source[None, None, :], 0), axis=2)
    recv_valid = jnp.any(wanted, axis=2)
    send_mask = send_valid[:, :, None, None].astype(jnp.bfloat16)
    embedded_own = jnp.dot(
        tokens.reshape(img_dev * patches, enc_width), w_embed, preferred_element_type=jnp.float32
    )
    embedded_own = embedded_own.astype(jnp.bfloat16).reshape(img_dev, patches, -1)
    outgoing = embedded_own[send_index] * send_mask
    received = lax.all_to_all(outgoing, "img", split_axis=0, concat_axis=0, tiled=True)
    pair_views = received.reshape(owners * slot_cap, patches, -1)[recv_index]

    def run_block(index_block, totals):
        first_row = index_block * PAIR_BLOCK
        block_views = lax.dynamic_slice_in_dim(pair_views, first_row, PAIR_BLOCK, 0)
        block_result = decode_block(block_views, w_query, w_key, w_value, w_out, w_head)
        return lax.dynamic_update_slice_in_dim(totals, block_result, first_row, 0)

    block_count = (my_share + PAIR_BLOCK - 1) // PAIR_BLOCK
    results = lax.fori_loop(
        0, block_count, run_block, jnp.zeros((pair_cap, 2, channels * patches), jnp.float32)
    )
    results = results * recv_valid[:, :, None].astype(jnp.float32)
    return_map = (
        jnp.arange(owners * slot_cap, dtype=jnp.int32)[:, None] == recv_index.reshape(1, -1)
    ) & recv_valid.reshape(1, -1)
    outgoing_back = jnp.dot(
        return_map.astype(jnp.float32),
        results.reshape(pair_cap * 2, -1),
        precision=lax.Precision.HIGHEST,
        preferred_element_type=jnp.float32,
    )
    returned = lax.all_to_all(
        outgoing_back.reshape(owners, slot_cap, -1), "img", split_axis=0, concat_axis=0, tiled=True
    )
    owner_map = (
        jnp.arange(img_dev, dtype=jnp.int32)[:, None] == send_index.reshape(1, -1)
    ) & send_valid.reshape(1, -1)
    owner_partial = jnp.dot(
        owner_map.astype(jnp.float32),
        returned.reshape(owners * slot_cap, -1),
        precision=lax.Precision.HIGHEST,
        preferred_element_type=jnp.float32,
    )
    totals = lax.psum(owner_partial, "grp")
    return join(totals, patches, channels)


def split3(values):
    high = values.astype(jnp.bfloat16)
    rest = values - high.astype(jnp.float32)
    middle = rest.astype(jnp.bfloat16)
    low = (rest - middle.astype(jnp.float32)).astype(jnp.bfloat16)
    return jnp.concatenate([high, middle, low], axis=0)


def sum3(values):
    part = values.shape[0] // 3
    return values[:part] + values[part : 2 * part] + values[2 * part :]


NT = (((1,), (1,)), ((), ()))


def decode(
    heads, source_ref, local_ref, normed_ref, query_ref, key_ref, value_ref, base_ref, place_ref,
    live_ref, out_ref, partner_rows, query_rows, attended
):
    ends = source_ref.shape[0]
    patches, width = normed_ref.shape[1:]
    channels = base_ref.shape[0]
    head_size = width // heads
    rows = ends * patches

    def fetch(end, carry):
        at = pl.ds(pl.multiple_of(end * patches, patches), patches)
        partner_rows[at, :] = normed_ref[source_ref[end]].astype(jnp.float32)
        return carry

    lax.fori_loop(0, ends, fetch, 0, unroll=8)

    chunk = min(256, rows)
    group = LANES
    side = LANES // head_size
    lane = lax.broadcasted_iota(jnp.int32, (group, LANES), 1)
    column = lax.broadcasted_iota(jnp.int32, (patches, side * group), 1)
    column_end = (column % group) // patches

    def one_chunk(index, carry):
        first = pl.multiple_of(index * chunk, chunk)
        partner = partner_rows[pl.ds(first, chunk), :].astype(jnp.bfloat16)
        keys = jnp.dot(partner, key_ref[...], preferred_element_type=jnp.float32)
        keys = keys.astype(jnp.bfloat16)
        values = lax.dot_general(
            value_ref[...], partner, NT, preferred_element_type=jnp.float32
        ).astype(jnp.bfloat16)
        for part in range(chunk // group):
            begin = part * group
            all_weights = []
            all_values = []
            for block in range(width // LANES):
                cols = slice(block * LANES, (block + 1) * LANES)
                asked = query_rows[pl.ds(first + begin, group), cols]
                stacked = jnp.concatenate(
                    [jnp.where(lane // head_size == s, asked, 0.0) for s in range(side)], axis=0
                ).astype(jnp.bfloat16)
                scores = lax.dot_general(
                    keys[begin : begin + group, cols], stacked, NT,
                    preferred_element_type=jnp.float32,
                )
                packed = jnp.zeros((patches, side * group), jnp.float32)
                for end in range(group // patches):
                    packed = jnp.where(
                        column_end == end, scores[end * patches : (end + 1) * patches], packed
                    )
                grown = jnp.exp(packed - jnp.max(packed, axis=0, keepdims=True))
                weights = grown / jnp.sum(grown, axis=0, keepdims=True)
                spread = jnp.concatenate(
                    [jnp.where(column_end == end, weights, 0.0) for end in range(group // patches)],
                    axis=0,
                ).astype(jnp.bfloat16)
                for s in range(side):
                    head = block * side + s
                    all_weights.append(spread[:, s * group : (s + 1) * group])
                    all_values.append(
                        values[head * channels : (head + 1) * channels, begin : begin + group]
                    )
            attended[:, pl.ds(pl.multiple_of(first + begin, group), group)] = jnp.dot(
                jnp.concatenate(all_values, axis=1),
                jnp.concatenate(all_weights, axis=0),
                preferred_element_type=jnp.float32,
            )
        return carry

    lax.fori_loop(0, rows // chunk, one_chunk, 0)

    own_rows = base_ref.shape[1]
    target = lax.broadcasted_iota(jnp.int32, (own_rows, rows), 0)
    owner_map = jnp.where(target == place_ref[...], 1.0, 0.0).astype(jnp.bfloat16)
    base = sum3(jnp.dot(split3(base_ref[...]), owner_map, preferred_element_type=jnp.float32))
    head_out = base + attended[...]
    confidence = 1.0 + jnp.exp(head_out[3:4, :])
    channel = lax.broadcasted_iota(jnp.int32, head_out.shape, 0)
    result = jnp.where(channel == 3, confidence, confidence * head_out)
    result = jnp.where(live_ref[...] > 0, result, 0.0)
    out_ref[...] = sum3(
        lax.dot_general(split3(result), owner_map, NT, preferred_element_type=jnp.float32)
    )


def gather_kernel(
    depth, heads, source_ref, local_ref, place_ref, live_ref, own_ref, normed_ref, embedded_ref,
    head_ref, query_hbm, out_hbm, value_hbm, key_hbm, totals_ref, all_ref, query_ref, value_ref,
    base_ref, partner_rows, query_rows, attended, weights, weight_sem, place_sem, send_sem,
    recv_sem, mate_send_sem, mate_recv_sem
):
    share = own_ref.shape[0]
    me = lax.axis_index("img")
    core = lax.axis_index("grp")
    layer = me // 4
    tall = me // 2 % 2
    wide = me % 2
    mesh_ids = pl.DeviceIdType.MESH
    loads = [
        pltpu.make_async_copy(source, weights.at[index], weight_sem.at[index])
        for index, source in enumerate((query_hbm, out_hbm, value_hbm, key_hbm))
    ]
    for load in loads:
        load.start()

    def own_queries():
        head_size = normed_ref.shape[1] // heads
        loads[0].wait()
        asked = jnp.dot(normed_ref[...], weights[0], preferred_element_type=jnp.float32)
        asked = asked.astype(jnp.bfloat16).astype(jnp.float32) / math.sqrt(head_size)
        query_ref[...] = asked.reshape(query_ref.shape)
        base_ref[...] = lax.dot_general(
            head_ref[...], embedded_ref[...], NT, preferred_element_type=jnp.float32
        )

    def place_queries():
        patches = query_ref.shape[1]

        def fetch(end, carry):
            at = pl.ds(pl.multiple_of(end * patches, patches), patches)
            query_rows[at, :] = query_ref[local_ref[end]]
            return carry

        lax.fori_loop(0, local_ref.shape[0], fetch, 0, unroll=8)

    def value_to_head():
        head_size = normed_ref.shape[1] // heads
        channels = head_ref.shape[0]
        loads[1].wait()
        out_head = lax.dot_general(
            head_ref[...], weights[1], NT, preferred_element_type=jnp.float32
        )
        tiled = jnp.concatenate([out_head] * heads, axis=0)
        row = lax.broadcasted_iota(jnp.int32, tiled.shape, 0)
        column = lax.broadcasted_iota(jnp.int32, tiled.shape, 1)
        tiled = jnp.where(row // channels == column // head_size, tiled, 0.0)
        high = tiled.astype(jnp.bfloat16)
        low = (tiled - high.astype(jnp.float32)).astype(jnp.bfloat16)
        loads[2].wait()
        value_ref[...] = (
            lax.dot_general(high, weights[2], NT, preferred_element_type=jnp.float32)
            + lax.dot_general(low, weights[2], NT, preferred_element_type=jnp.float32)
        ).astype(jnp.bfloat16)

    def chip(z, y, x):
        return z * 4 + y * 2 + x

    def slot(unit):
        return all_ref.at[pl.ds((unit * 2 + core) * share, share)]

    def copy(unit, way, target, source=None):
        return pltpu.make_async_remote_copy(
            src_ref=slot(unit) if source is None else source,
            dst_ref=slot(unit),
            send_sem=send_sem.at[way, unit],
            recv_sem=recv_sem.at[unit],
            device_id={"img": target, "grp": core},
            device_id_type=mesh_ids,
        )

    def mate_copy(unit, source=None):
        return pltpu.make_async_remote_copy(
            src_ref=slot(unit) if source is None else source,
            dst_ref=slot(unit),
            send_sem=mate_send_sem.at[unit],
            recv_sem=mate_recv_sem.at[unit],
            device_id={"img": me, "grp": 1 - core},
            device_id_type=mesh_ids,
        )

    across = chip(layer, tall, 1 - wide)
    along = chip(layer, 1 - tall, wide)
    has = {1: layer < depth - 1, -1: layer > 0}

    barrier = pltpu.get_barrier_semaphore()
    for target in (across, along):
        pl.semaphore_signal(
            barrier, inc=1, device_id={"img": target, "grp": core}, device_id_type=mesh_ids
        )
    pl.semaphore_signal(
        barrier, inc=1, device_id={"img": me, "grp": 1 - core}, device_id_type=mesh_ids
    )
    for sign in (1, -1):
        @pl.when(has[sign])
        def _():
            pl.semaphore_signal(
                barrier,
                inc=1,
                device_id={"img": me + 4 * sign, "grp": core},
                device_id_type=mesh_ids,
            )
    pl.semaphore_wait(
        barrier, 3 + has[1].astype(jnp.int32) + has[-1].astype(jnp.int32)
    )

    def run(action, between):
        def at(distance, sign, body):
            z = layer + sign * distance
            if distance == 0:
                body(z)
            else:
                pl.when((z >= 0) & (z < depth))(lambda: body(z))

        for step in range(depth + 2):
            for sign in (1, -1):
                if step < depth and (step > 0 or sign == 1):
                    def column(z):
                        unit = chip(z, tall, wide)
                        own = own_ref if step == 0 else None
                        if step > 0:
                            action("arrive", lambda: copy(unit, 0, across))
                        for onward in (1, -1):
                            if step == 0 or onward == -sign:
                                @pl.when(has[onward])
                                def _():
                                    action(
                                        "send",
                                        lambda: copy(unit, 0 if onward == 1 else 1, me + 4 * onward, own),
                                    )
                        action("send", lambda: copy(unit, 2, across, own))
                        action("send", lambda: copy(unit, 3, along, own))
                        action("send", lambda: mate_copy(unit, own))

                    at(step, sign, column)
                back = step - 1
                if 0 <= back < depth and (back > 0 or sign == 1):
                    def beside(z):
                        unit = chip(z, tall, 1 - wide)
                        action("arrive", lambda: copy(unit, 0, across))
                        @pl.when(z % 2 == 1)
                        def _():
                            action("send", lambda: copy(unit, 3, along))
                        action("send", lambda: mate_copy(unit))
                        unit_up = chip(z, 1 - tall, wide)
                        action("arrive", lambda: copy(unit_up, 0, across))
                        @pl.when(z % 2 == 0)
                        def _():
                            action("send", lambda: copy(unit_up, 2, across))
                        action("send", lambda: mate_copy(unit_up))

                    at(back, sign, beside)
                back2 = step - 2
                if 0 <= back2 < depth and (back2 > 0 or sign == 1):
                    def opposite(z):
                        unit = chip(z, 1 - tall, 1 - wide)
                        action("arrive", lambda: copy(unit, 0, across))
                        action("send", lambda: mate_copy(unit))

                    at(back2, sign, opposite)
            if step in between:
                between[step]()

    def begin(kind, descriptor):
        if kind == "send":
            descriptor().start()
        else:
            descriptor().wait_recv()

    def finish(kind, descriptor):
        if kind == "send":
            descriptor().wait_send()

    place = pltpu.make_async_copy(own_ref, slot(me), place_sem)
    place.start()
    run(begin, {0: own_queries, 1: value_to_head, 2: place_queries})
    run(finish, {})
    place.wait()

    def from_mate(unit, carry):
        theirs = all_ref.at[pl.ds((unit * 2 + 1 - core) * share, share)]
        pltpu.make_async_remote_copy(
            src_ref=theirs,
            dst_ref=theirs,
            send_sem=mate_send_sem.at[unit],
            recv_sem=mate_recv_sem.at[unit],
            device_id={"img": me, "grp": 1 - core},
            device_id_type=mesh_ids,
        ).wait_recv()
        return carry

    lax.fori_loop(0, 4 * depth, from_mate, 0)
    loads[3].wait()
    decode(
        heads, source_ref, local_ref, all_ref, query_ref, weights.at[3], value_ref, base_ref,
        place_ref, live_ref, totals_ref, partner_rows, query_rows, attended
    )


def gather_and_decode(
    owners, source, local, place, live_rows, outgoing, normed, embedded, head_weight, w_query,
    w_out, w_value, w_key
):
    share, patches, width = outgoing.shape
    wide = head_weight.shape[0]
    rows = place.shape[1]
    smem = pl.BlockSpec(memory_space=pltpu.SMEM)
    vmem = pl.BlockSpec(memory_space=pltpu.VMEM)
    away = pl.BlockSpec(memory_space=pl.ANY)
    return pl.pallas_call(
        functools.partial(gather_kernel, owners // 4, HEADS),
        out_shape=jax.ShapeDtypeStruct((wide, normed.shape[0]), jnp.float32),
        in_specs=[smem] * 2 + [vmem] * 6 + [away] * 4,
        out_specs=vmem,
        scratch_shapes=[
            pltpu.VMEM((owners * 2 * share, patches, width), outgoing.dtype),
            pltpu.VMEM((normed.shape[0] // patches, patches, width), jnp.float32),
            pltpu.VMEM((HEADS * wide, width), jnp.bfloat16),
            pltpu.VMEM((wide, normed.shape[0]), jnp.float32),
            pltpu.VMEM((rows, width), jnp.float32),
            pltpu.VMEM((rows, width), jnp.float32),
            pltpu.VMEM((wide, rows), jnp.float32),
            pltpu.VMEM((4, width, width), jnp.bfloat16),
            pltpu.SemaphoreType.DMA((4,)),
            pltpu.SemaphoreType.DMA,
            pltpu.SemaphoreType.DMA((4, owners)),
            pltpu.SemaphoreType.DMA((owners,)),
            pltpu.SemaphoreType.DMA((owners,)),
            pltpu.SemaphoreType.DMA((owners,)),
        ],
        compiler_params=pltpu.CompilerParams(
            collective_id=0, has_side_effects=True, vmem_limit_bytes=48 * 2**20
        ),
    )(
        source, local, place, live_rows, outgoing, normed, embedded, head_weight, w_query, w_out,
        w_value, w_key
    )


def look_up(owner_row, ids, img_dev):
    span = min(TABLE, owner_row.shape[0])
    table = owner_row.reshape(-1, span)
    parts = jnp.concatenate([table // img_dev, table % img_dev], axis=0).astype(jnp.bfloat16)
    hot = ids[None, :] % span == jnp.arange(span, dtype=jnp.int32)[:, None]
    found = jnp.dot(parts, hot.astype(jnp.bfloat16), preferred_element_type=jnp.float32)
    found = found.reshape(2, -1, ids.shape[0])
    pick = jnp.arange(found.shape[1], dtype=jnp.int32)[:, None] == ids[None, :] // span
    found = jnp.sum(jnp.where(pick[None], found, 0.0), axis=1).astype(jnp.int32)
    return found[0], found[1]


def by_owner(
    tokens, w_embed, w_query, w_key, w_value, w_out, w_head, pair_images, pair_counts, owner_row
):
    img_dev, patches, enc_width = tokens.shape
    dec_width, channels = w_head.shape
    owners = lax.axis_size("img")
    groups = lax.axis_size("grp")
    pair_cap = pair_images.shape[2]
    my_chip = lax.axis_index("img")
    my_group = lax.axis_index("grp")
    own_rows = img_dev * patches
    share = img_dev // groups
    embedded = jnp.dot(
        tokens.reshape(own_rows, enc_width), w_embed, preferred_element_type=jnp.float32
    ).astype(jnp.bfloat16)
    normed = layer_norm(embedded.astype(jnp.float32)).astype(jnp.bfloat16)
    outgoing = lax.dynamic_slice_in_dim(
        normed.reshape(img_dev, patches, dec_width), my_group * share, share, 0
    )
    wide = -(-channels // 8) * 8
    head_weight = jnp.pad(w_head.T, ((0, wide - channels), (0, 0)))

    end_count = groups * pair_cap * 2
    sides = [pair_images[..., s].reshape(owners, groups * pair_cap) for s in range(2)]
    ids = jnp.concatenate(sides, axis=1)
    owner, local = look_up(owner_row, ids.reshape(-1), img_dev)
    owner = owner.reshape(owners, end_count)
    local = local.reshape(owners, end_count)
    image_row = owner * img_dev + local
    half = end_count // 2
    partner = jnp.concatenate([image_row[:, half:], image_row[:, :half]], axis=1)
    live = jnp.arange(pair_cap, dtype=jnp.int32)[None, None, :] < pair_counts[:, :, None]
    live = live.reshape(owners, half).astype(jnp.int32)
    live = jnp.concatenate([live, live], axis=1)
    packed = (partner * img_dev + local) * 2 + live
    mine = owner == my_chip
    end_index = jnp.arange(end_count, dtype=jnp.int32)
    earlier = (end_index[:, None] < end_index[None, :]).astype(jnp.bfloat16)
    ranked = jnp.dot(mine.astype(jnp.bfloat16), earlier, preferred_element_type=jnp.float32)
    slot_cap = end_count // owners // groups
    slot = my_group * slot_cap + jnp.arange(slot_cap, dtype=jnp.int32)
    matched = mine[:, None, :] & (ranked.astype(jnp.int32)[:, None, :] == slot[None, :, None])
    chosen = jnp.sum(jnp.where(matched, packed[:, None, :], 0), axis=2).reshape(-1)
    ends = chosen.shape[0]
    chosen_live = chosen % 2
    chosen_local = (chosen // 2) % img_dev
    chosen_partner = chosen // (2 * img_dev)
    place = chosen_local[:, None] * patches + jnp.arange(patches, dtype=jnp.int32)[None, :]
    live_rows = jnp.broadcast_to(chosen_live[:, None], (ends, patches)).reshape(1, -1)

    totals = gather_and_decode(
        owners, chosen_partner, chosen_local, place.reshape(1, -1), live_rows, outgoing, normed,
        embedded, head_weight, w_query, w_out, w_value, w_key
    )
    totals = lax.psum(totals, "grp")
    totals = totals[:channels].reshape(channels, img_dev, patches).transpose(1, 0, 2)
    return join(totals, patches, channels)


def per_device(tokens, w_embed, w_query, *others):
    images = tokens.shape[0] * lax.axis_size("img")
    gathered = images * tokens.shape[1] * w_query.shape[0] * 2
    run = by_owner if gathered <= GATHER_LIMIT else by_executor
    return run(tokens, w_embed, w_query, *others)


def solution(mesh):
    in_specs = (P("img", None, None), P(), P(), P(), P(), P(), P(), P(), P(), P())
    out_specs = (P("img", None), P("img", None))
    return jax.shard_map(
        per_device, mesh=mesh, in_specs=in_specs, out_specs=out_specs, check_vma=False
    )
```
